256 devices in a mesh: rows: 16 (over x, z_hi), cols: 16 (over y, z_lo, core).
Axes of the slice: x: 4, y: 4, z: 8 (z_hi: 4, z_lo: 2; z = z_hi * 2 + z_lo), core: 2. Of those that a mesh axis runs over, the one named last changes fastest.
Arguments:
- features: bfloat16 [512, 512, 128], P('rows', 'cols'), may hold values from -6 to 6
- cotangent: bfloat16 [512, 512, 128], P('rows', 'cols'), may hold values from -6 to 6
- weight: bfloat16 [512, 512], replicated, may hold values from -0.25 to 0.25
- degree: int32 [512, 128], P('rows'), may hold values from 16 to 128
- tile_row: int32 [4096], P('rows'), may hold values from 0 to 31
- tile_col: int32 [4096], P('rows'), may hold values from 0 to 511, as said below
- tile_count: int32 [16], P('rows'), may hold values from 64 to 256, as said below
- tile_weights: bfloat16 [4096, 128, 128], P('rows'), may hold values from 0 to 3
Outputs:
- activated: bfloat16 [512, 512, 128], P('rows', 'cols')
- input_grad: bfloat16 [512, 512, 128], P('rows', 'cols')
- weight_grad: float32 [512, 512], P('cols')
The draws below stay inside these ranges and needn't reach their ends.
Inputs may be any that keep to these rules, and one draw needn't show every extreme that they name: `tile_col`: within each owner's 256 slots the column blocks never fall. `tile_count`: each owner has 256, 128 or 64 live slots, the first ones of its range; some owner has 256.
All inputs are finite; a program needn't handle non-finite values.
Results may differ from the reference program's by a relative error of at most 0.019.
Values may be sent and summed in bfloat16 or wider, within the bound.
A program may use at most 64 MiB of HBM per device.

```python
import jax
import jax.numpy as jnp
from jax import lax

F = 512
BLK = 128
NB_DEV = 32
T_DEV = 256
OWNERS = 16
NODE_BLOCKS = 512
TILES = 4096


def draw_tile_count(key, part):
    key = jax.random.fold_in(key, 12)
    first_key, second_key = jax.random.split(key)
    halvings = jax.random.randint(first_key, (OWNERS,), 0, 3, jnp.int32)
    counts = jnp.right_shift(jnp.full((OWNERS,), T_DEV, jnp.int32), halvings)
    forced = jax.random.randint(second_key, (), 0, OWNERS, jnp.int32)
    return jnp.where(jnp.arange(OWNERS, dtype=jnp.int32) == forced, jnp.int32(T_DEV), counts)


def draw_tile_col(key, part):
    key = jax.random.fold_in(key, 13)
    picked = jax.random.randint(key, (OWNERS, T_DEV), 0, NODE_BLOCKS, jnp.int32)
    return jnp.sort(picked, axis=1).reshape(TILES)


def touch_ends(drawn, key, least, high):
    spot = [jax.random.randint(jax.random.fold_in(key, axis), (), 0, length) for axis, length in enumerate(drawn.shape)]
    widest = drawn.shape.index(max(drawn.shape))
    next_to = spot[:widest] + [(spot[widest] + 1) % drawn.shape[widest]] + spot[widest + 1:]
    return drawn.at[tuple(spot)].set(least).at[tuple(next_to)].set(high)


def block_levels(rng, extent, shards, low, largest):
    def one(position, blocks):
        draws = jax.random.uniform(jax.random.fold_in(jax.random.fold_in(rng, 6), position), (blocks,), jnp.float32, low / len(shards), largest / len(shards))
        return jnp.repeat(jnp.exp(draws), extent[position] // blocks).reshape((-1,) + (1,) * (len(extent) - position - 1))

    loudness = one(*shards[0])
    for cut in shards[1:]:
        loudness = loudness * one(*cut)
    return loudness


def centred(key, shape, width, most, cuts=(), held_as=jnp.bfloat16):
    values = width * jax.random.normal(key, shape, jnp.float32)
    if cuts:
        values = values * block_levels(key, shape, cuts, -0.22, 0.18)
    return jnp.clip(values, -most, most).astype(held_as)


def setup_inputs(seed: int = 0) -> dict:
    streams_of = jax.random.split(jax.random.key(seed), 9)
    return {
        "features": centred(streams_of[0], (NODE_BLOCKS, F, BLK), 1.0, 6.0, ((0, 16), (1, 16))),
        "cotangent": centred(streams_of[1], (NODE_BLOCKS, F, BLK), 1.0, 6.0, ((0, 16), (1, 16))),
        "weight": centred(streams_of[2], (F, F), F ** -0.5, 0.25),
        "degree": touch_ends(jax.random.randint(streams_of[3], (NODE_BLOCKS, BLK), 16, 129), jax.random.fold_in(streams_of[3], 1), 16, 128).astype(jnp.int32),
        "tile_row": touch_ends(jax.random.randint(streams_of[4], (TILES,), 0, NB_DEV), jax.random.fold_in(streams_of[4], 1), 0, NB_DEV - 1).astype(jnp.int32),
        "tile_col": draw_tile_col(jax.random.fold_in(streams_of[8], 71), 0),
        "tile_count": draw_tile_count(jax.random.fold_in(streams_of[8], 71), 0),
        "tile_weights": jnp.clip(3.0 * jax.random.uniform(streams_of[7], (TILES, BLK, BLK), jnp.float32) ** block_levels(streams_of[7], (TILES, BLK, BLK), ((0, 16),), -0.2, 0.2), 0.0, 3.0).astype(jnp.bfloat16),
    }


def reference(features, cotangent, weight, degree, tile_row, tile_col, tile_count, tile_weights):
    scale = lax.rsqrt(degree.astype(jnp.float32))
    scaled = (features.astype(jnp.float32) * scale[:, None, :]).astype(jnp.bfloat16)
    tile_block = min(64, T_DEV)
    order = jnp.arange(tile_block, dtype=jnp.int32)
    highest = lax.Precision.HIGHEST

    def tile_slices(owner, index):
        first = (owner * T_DEV + index * tile_block).astype(jnp.int32)
        adjacency = lax.dynamic_slice_in_dim(tile_weights, first, tile_block, 0)
        row_ids = lax.dynamic_slice_in_dim(tile_row, first, tile_block, 0)
        col_ids = lax.dynamic_slice_in_dim(tile_col, first, tile_block, 0)
        alive = (index * tile_block + order < tile_count[owner]).astype(jnp.float32)
        return (adjacency.astype(jnp.float32), row_ids, col_ids, alive)

    def owner_forward(owner):

        def advance(index, running):
            adjacency, row_ids, col_ids, alive = tile_slices(owner, index)
            blocks = jnp.take(scaled, col_ids, axis=0).astype(jnp.float32)
            message = jnp.einsum('tfj,tij->tfi', blocks, adjacency, precision=highest)
            select = (row_ids[None, :] == jnp.arange(NB_DEV, dtype=jnp.int32)[:, None]).astype(jnp.float32) * alive[None, :]
            return running + jnp.einsum('bt,tfi->bfi', select, message, precision=highest)
        upper = (tile_count[owner] + tile_block - 1) // tile_block
        return lax.fori_loop(0, upper, advance, jnp.zeros((NB_DEV, F, BLK), jnp.float32))
    aggregated = lax.map(owner_forward, jnp.arange(OWNERS, dtype=jnp.int32)).reshape(NODE_BLOCKS, F, BLK)
    hidden = (aggregated * scale[:, None, :]).astype(jnp.bfloat16)
    hidden_wide = hidden.astype(jnp.float32)
    weight_wide = weight.astype(jnp.float32)
    pre = jnp.einsum('bfn,fo->bon', hidden_wide, weight_wide, precision=highest)
    activated = jax.nn.silu(pre).astype(jnp.bfloat16)
    sigmoid_pre = jax.nn.sigmoid(pre)
    slope = (cotangent.astype(jnp.float32) * sigmoid_pre * (1.0 + pre * (1.0 - sigmoid_pre))).astype(jnp.bfloat16)
    slope_wide = slope.astype(jnp.float32)
    weight_grad = jnp.einsum('bfn,bon->fo', hidden_wide, slope_wide, precision=highest)
    back_sum = jnp.einsum('fo,bon->bfn', weight_wide, slope_wide, precision=highest)
    back = (back_sum * scale[:, None, :]).astype(jnp.bfloat16)

    def owner_backward(owner, spread):
        owner_rows = lax.dynamic_slice_in_dim(back, (owner * NB_DEV).astype(jnp.int32), NB_DEV, 0)

        def advance(index, running):
            adjacency, row_ids, col_ids, alive = tile_slices(owner, index)
            blocks = jnp.take(owner_rows, row_ids, axis=0).astype(jnp.float32)
            contrib = jnp.einsum('tfi,tij->tfj', blocks, adjacency, precision=highest) * alive[:, None, None]
            return running.at[col_ids].add(contrib)
        upper = (tile_count[owner] + tile_block - 1) // tile_block
        return lax.fori_loop(0, upper, advance, spread)
    spread = lax.fori_loop(0, OWNERS, lambda owner, carried: owner_backward(jnp.int32(owner), carried), jnp.zeros((NODE_BLOCKS, F, BLK), jnp.float32))
    input_grad = (spread * scale[:, None, :]).astype(jnp.bfloat16)
    return (activated, input_grad, weight_grad)
```

```python
import functools

import jax
import jax.numpy as jnp
from jax import lax
from jax.experimental import pallas as pl
from jax.experimental.pallas import tpu as pltpu
from jax.sharding import PartitionSpec as P

BF = jnp.bfloat16
F32 = jnp.float32
NB = 32
FS = 32
BLK = 128
NX = 4
NZ = 4
NR = NX * NZ
NY = 4
NC = 16
ZFIRST = 24
TB = 16


def rank_along(axis, step):
    r = lax.axis_index("rows")
    x, z = r // NZ, r % NZ
    if axis == "x":
        return ((x + step + NX) % NX) * NZ + z
    return x * NZ + (z + step + NZ) % NZ


def owner_at(first, a, second, b):
    r = lax.axis_index("rows")
    step = {first: a, second: b}
    return ((r // NZ + step["x"] + NX) % NX) * NZ + (r % NZ + step["z"] + NZ) % NZ


class Copies:
    def __init__(self, send, recv):
        self.send, self.recv, self.n, self.started = send, recv, 0, []

    def start(self, src, dst, device):
        k = self.n
        self.n += 1
        c = pltpu.make_async_remote_copy(
            src_ref=src,
            dst_ref=dst,
            send_sem=self.send.at[k],
            recv_sem=self.recv.at[k],
            device_id=device,
            device_id_type=pl.DeviceIdType.MESH,
        )
        c.start()
        self.started.append(c)
        return c

    def finish(self):
        for c in self.started:
            c.wait_send()


def greet(devices):
    barrier = pltpu.get_barrier_semaphore()
    for d in devices:
        pl.semaphore_signal(barrier, inc=1, device_id=d, device_id_type=pl.DeviceIdType.MESH)
    pl.semaphore_wait(barrier, len(devices))


def other_cols():
    c = lax.axis_index("cols")
    return [{"cols": (c + k) % NC} for k in range(1, NC)]


def gather_kernel(feat, deg, cot, w, out, wt, cotx, own, send, recv, lsem):
    me = lax.axis_index("rows")
    c = lax.axis_index("cols")
    peers = [{"rows": rank_along(a, s)} for a in ("x", "z") for s in (1, -1)]
    greet(peers + other_cols())
    copies = Copies(send, recv)

    def scale_block(b, carry):
        s = lax.rsqrt(deg[pl.ds(b, 1), :].astype(F32))
        own[b] = (feat[b].astype(F32) * s).astype(BF)
        return carry

    lax.fori_loop(0, NB, scale_block, 0)
    local = pltpu.make_async_copy(own, out.at[pl.ds(me * NB, NB)], lsem.at[0])
    local.start()

    class Group:
        def __init__(self, first, second, lo, n):
            self.f, self.s, self.lo, self.n = first, second, lo, n

        def blocks(self, a, b, lo, n):
            return pl.ds(owner_at(self.f, a, self.s, b) * NB + self.lo + lo, n)

        def push(self, a, b, lo, n, axis, step):
            ds = self.blocks(a, b, lo, n)
            src = own.at[pl.ds(self.lo + lo, n)] if (a, b) == (0, 0) else out.at[ds]
            return copies.start(src, out.at[ds], {"rows": rank_along(axis, step)})

        def first_start(self):
            self.a_up = self.push(0, 0, 0, self.n, self.f, 1)
            self.a_dn = self.push(0, 0, 0, self.n, self.f, -1)

        def second_start(self, a, lo, n):
            return [a, lo, n, self.push(a, 0, lo, n, self.s, 1), self.push(a, 0, lo, n, self.s, -1)]

        def second_forward(self, item):
            a, lo, n, up, dn = item
            h = n // 2
            up.wait_recv()
            u = self.push(a, -1, lo, h, self.s, 1)
            dn.wait_recv()
            d = self.push(a, 1, lo + h, n - h, self.s, -1)
            return [u, d]

        def first_forward(self):
            h = self.n // 2
            self.a_up.wait_recv()
            self.f_up = self.push(-1, 0, 0, h, self.f, 1)
            self.a_dn.wait_recv()
            self.f_dn = self.push(1, 0, h, self.n - h, self.f, -1)

    gp = Group("z", "x", 0, ZFIRST)
    gq = Group("x", "z", ZFIRST, NB - ZFIRST)
    last = []
    gp.first_start()
    gq.first_start()
    p0 = gp.second_start(0, 0, gp.n)
    q0 = gq.second_start(0, 0, gq.n)
    arrivals = []
    for k, dev in enumerate(other_cols(), 1):
        arrivals.append(copies.start(cot.at[pl.ds(2 * ((c + k) % NC), 2)], cotx.at[c], dev))
    keep = pltpu.make_async_copy(cot.at[pl.ds(2 * c, 2)], cotx.at[c], lsem.at[1])
    keep.start()
    wt[...] = w[...].T
    gq.first_forward()
    gp.first_forward()
    pu = gp.second_start(-1, 0, gp.n)
    pd = gp.second_start(1, 0, gp.n)
    last += gp.second_forward(p0)
    qu = gq.second_start(-1, 0, gq.n)
    qd = gq.second_start(1, 0, gq.n)
    last += gq.second_forward(q0)
    for g, pair in ((gq, []), (gp, [])):
        h = g.n // 2
        g.f_up.wait_recv()
        g.i_up = g.second_start(-2, 0, h)
        g.f_dn.wait_recv()
        g.i_dn = g.second_start(2, h, g.n - h)
    last += gp.second_forward(pu)
    last += gp.second_forward(pd)
    last += gq.second_forward(qu)
    last += gq.second_forward(qd)
    last += gq.second_forward(gq.i_up)
    last += gq.second_forward(gq.i_dn)
    last += gp.second_forward(gp.i_up)
    last += gp.second_forward(gp.i_dn)
    for cp in last + arrivals:
        cp.wait_recv()
    local.wait()
    keep.wait()
    copies.finish()


N_GATHER = 2 * (2 + 2 + 10 + 10) + NC - 1


def gather_rows(features, degree, cotangent, weight):
    vm = pl.BlockSpec(memory_space=pltpu.VMEM)
    hb = pl.BlockSpec(memory_space=pl.ANY)
    return pl.pallas_call(
        gather_kernel,
        name="gather_rows",
        out_shape=(
            jax.ShapeDtypeStruct((NR * NB, FS, BLK), BF),
            jax.ShapeDtypeStruct(weight.shape, BF),
            jax.ShapeDtypeStruct((NC, 2, FS, BLK), BF),
        ),
        in_specs=[vm, vm, hb, vm],
        out_specs=(hb, vm, hb),
        scratch_shapes=[
            pltpu.VMEM((NB, FS, BLK), BF),
            pltpu.SemaphoreType.DMA((N_GATHER,)),
            pltpu.SemaphoreType.DMA((N_GATHER,)),
            pltpu.SemaphoreType.DMA((2,)),
        ],
        compiler_params=pltpu.CompilerParams(
            collective_id=0, has_side_effects=True, vmem_limit_bytes=24 << 20
        ),
    )(features, degree, cotangent, weight)


def aggregate_kernel(col, row, count, gathered, deg, a, hidden, acc):
    step = pl.program_id(0)

    @pl.when(step == 0)
    def _():
        acc[...] = jnp.zeros_like(acc)

    @pl.when(step * TB < count[0])
    def _():
        for k in range(TB):
            t = step * TB + k
            m = lax.dot_general(
                gathered[col[t]], a[k], (((1,), (1,)), ((), ())), preferred_element_type=F32
            )
            acc[row[t]] += m

    @pl.when(step == pl.num_programs(0) - 1)
    def _():
        for b in range(NB):
            s = lax.rsqrt(deg[pl.ds(b, 1), :].astype(F32))
            hidden[b] = (acc[b] * s).astype(BF)


def last_live(i, count):
    return jnp.minimum(i, (count[0] + TB - 1) // TB - 1)


def aggregate(gathered, degree, tile_col, tile_row, tile_count, tile_weights):
    tiles = tile_col.shape[0]
    return pl.pallas_call(
        aggregate_kernel,
        name="aggregate",
        out_shape=jax.ShapeDtypeStruct((NB, FS, BLK), BF),
        grid_spec=pltpu.PrefetchScalarGridSpec(
            num_scalar_prefetch=3,
            grid=(tiles // TB,),
            in_specs=[
                pl.BlockSpec((NR * NB, FS, BLK), lambda i, *_: (0, 0, 0)),
                pl.BlockSpec((NB, BLK), lambda i, *_: (0, 0)),
                pl.BlockSpec((TB, BLK, BLK), lambda i, c, r, n: (last_live(i, n), 0, 0)),
            ],
            out_specs=pl.BlockSpec((NB, FS, BLK), lambda i, *_: (0, 0, 0)),
            scratch_shapes=[pltpu.VMEM((NB, FS, BLK), F32)],
        ),
        compiler_params=pltpu.CompilerParams(vmem_limit_bytes=32 << 20),
    )(tile_col, tile_row, tile_count, gathered, degree, tile_weights)


def dense_kernel(hid, cotx, w, wt, deg, act, back, wg, hx, act_s, back_s, send, recv, lsem):
    c = lax.axis_index("cols")
    devs = other_cols()
    greet(devs)
    copies = Copies(send, recv)
    arrivals = [
        copies.start(hid.at[pl.ds(2 * ((c + k) % NC), 2)], hx.at[c], dev)
        for k, dev in enumerate(devs, 1)
    ]
    hx[c] = hid[pl.ds(2 * c, 2)]
    for cp in arrivals:
        cp.wait_recv()

    def wide(ref):
        return jnp.concatenate([ref[:, 0].reshape(NC * FS, BLK), ref[:, 1].reshape(NC * FS, BLK)], axis=1)

    def narrow(ref, value):
        for b in range(2):
            ref[:, b] = value[:, b * BLK : (b + 1) * BLK].reshape(NC, FS, BLK)

    def spread_out(src, dst, sem):
        got = [
            copies.start(src.at[(c + k) % NC], dst.at[pl.ds(2 * c, 2)], dev)
            for k, dev in enumerate(devs, 1)
        ]
        mine = pltpu.make_async_copy(src.at[c], dst.at[pl.ds(2 * c, 2)], sem)
        mine.start()
        return got, mine

    x = wide(hx)
    pre = jnp.dot(wt[...], x, preferred_element_type=F32)
    sig = jax.nn.sigmoid(pre)
    narrow(act_s, (pre * sig).astype(BF))
    got_a, mine_a = spread_out(act_s, act, lsem.at[0])
    slope = (wide(cotx).astype(F32) * sig * (1.0 + pre * (1.0 - sig))).astype(BF)
    s = jnp.concatenate(
        [lax.rsqrt(deg[pl.ds(2 * c + b, 1), :].astype(F32)) for b in range(2)], axis=1
    )
    bk = jnp.dot(w[...], slope, preferred_element_type=F32) * s
    narrow(back_s, bk.astype(BF))
    got_b, mine_b = spread_out(back_s, back, lsem.at[1])
    wg[...] = (
        lax.dot_general(x, slope, (((1,), (1,)), ((), ())), preferred_element_type=F32)
        .astype(BF)
        .reshape(wg.shape)
    )
    for cp in got_a + got_b:
        cp.wait_recv()
    mine_a.wait()
    mine_b.wait()
    copies.finish()


def dense(hidden, cotx, weight, wt, degree):
    vm = pl.BlockSpec(memory_space=pltpu.VMEM)
    hb = pl.BlockSpec(memory_space=pl.ANY)
    n = 3 * (NC - 1)
    return pl.pallas_call(
        dense_kernel,
        name="dense",
        out_shape=(
            jax.ShapeDtypeStruct((NB, FS, BLK), BF),
            jax.ShapeDtypeStruct((NB, FS, BLK), BF),
            jax.ShapeDtypeStruct((NC, FS, weight.shape[1]), BF),
        ),
        in_specs=[vm] * 5,
        out_specs=(hb, hb, vm),
        scratch_shapes=[
            pltpu.VMEM((NC, 2, FS, BLK), BF),
            pltpu.VMEM((NC, 2, FS, BLK), BF),
            pltpu.VMEM((NC, 2, FS, BLK), BF),
            pltpu.SemaphoreType.DMA((n,)),
            pltpu.SemaphoreType.DMA((n,)),
            pltpu.SemaphoreType.DMA((2,)),
        ],
        compiler_params=pltpu.CompilerParams(
            collective_id=1, has_side_effects=True, vmem_limit_bytes=24 << 20
        ),
    )(hidden, cotx, weight, wt, degree)


def spread_kernel(col, row, count, back, a, out, acc):
    step = pl.program_id(0)

    @pl.when(step == 0)
    def _():
        out[...] = jnp.zeros_like(out)
        acc[...] = jnp.zeros_like(acc)

    @pl.when(step * TB < count[0])
    def _():
        run = acc[...]
        for k in range(TB):
            t = step * TB + k
            m = jnp.dot(back[row[t]], a[k], preferred_element_type=F32)
            same = col[t] == col[jnp.maximum(t - 1, 0)]
            run = jnp.where(same, run, 0.0) + m
            out[col[t]] = run.astype(BF)
        acc[...] = run


def spread(back, tile_col, tile_row, tile_count, tile_weights):
    tiles = tile_col.shape[0]
    return pl.pallas_call(
        spread_kernel,
        name="spread",
        out_shape=jax.ShapeDtypeStruct((NR * NB, FS, BLK), BF),
        grid_spec=pltpu.PrefetchScalarGridSpec(
            num_scalar_prefetch=3,
            grid=(tiles // TB,),
            in_specs=[
                pl.BlockSpec((NB, FS, BLK), lambda i, *_: (0, 0, 0)),
                pl.BlockSpec((TB, BLK, BLK), lambda i, c, r, n: (last_live(i, n), 0, 0)),
            ],
            out_specs=pl.BlockSpec((NR * NB, FS, BLK), lambda i, *_: (0, 0, 0)),
            scratch_shapes=[pltpu.VMEM((FS, BLK), F32)],
        ),
        compiler_params=pltpu.CompilerParams(vmem_limit_bytes=32 << 20),
    )(tile_col, tile_row, tile_count, back, tile_weights)


def scatter_kernel(
    part, deg, wg, out, wout, inner, summed, half, tail, wy, ws, wc, wm, wz, w1, wx, w2, wv, send, recv
):
    c = lax.axis_index("cols")
    y, low = c // 4, c % 4
    zl, core = low // 2, low % 2
    ypeers = [{"cols": ((y + k) % NY) * 4 + low} for k in range(1, NY)]
    cpeer = {"cols": c + 1 - 2 * core}
    zpeer = {"cols": c + 2 - 4 * zl}
    xs = [{"rows": rank_along("x", k)} for k in range(1, NX)]
    zs = [{"rows": rank_along("z", k)} for k in range(1, NZ)]
    greet(ypeers + [cpeer, zpeer] + xs + zs)
    copies = Copies(send, recv)

    class Group:
        def __init__(self, first, second, lo, n):
            self.f, self.s, self.lo, self.n = first, second, lo, n

        def local(self, a, b):
            return part.at[pl.ds(owner_at(self.f, a, self.s, b) * NB + self.lo, self.n)]

    def ring_start(axis, n, shard, land):
        h = n // 2
        up, dn = {"rows": rank_along(axis, 1)}, {"rows": rank_along(axis, -1)}
        return {
            "n": n,
            "up": up,
            "dn": dn,
            "shard": shard,
            "land": land,
            "far_dn": copies.start(shard(-2).at[pl.ds(0, h)], land.at[pl.ds(0, h)], dn),
            "far_up": copies.start(shard(2).at[pl.ds(h, n - h)], land.at[pl.ds(h, n - h)], up),
            "raw_dn": copies.start(shard(-1).at[pl.ds(h, n - h)], land.at[pl.ds(n + h, n - h)], dn),
            "raw_up": copies.start(shard(1).at[pl.ds(0, h)], land.at[pl.ds(2 * n, h)], up),
        }

    def add_into(dst, a, b):
        def one(i, carry):
            dst[i] = (a[i].astype(F32) + b[i].astype(F32)).astype(BF)
            return carry

        lax.fori_loop(0, dst.shape[0], one, 0, unroll=2)

    def ring_forward(r, work):
        n, land = r["n"], r["land"]
        h = n // 2
        r["far_dn"].wait_recv()
        add_into(work.at[pl.ds(0, h)], land.at[pl.ds(0, h)], r["shard"](-1).at[pl.ds(0, h)])
        r["sum_dn"] = copies.start(work.at[pl.ds(0, h)], land.at[pl.ds(n, h)], r["dn"])
        r["far_up"].wait_recv()
        add_into(
            work.at[pl.ds(h, n - h)], land.at[pl.ds(h, n - h)], r["shard"](1).at[pl.ds(h, n - h)]
        )
        r["sum_up"] = copies.start(work.at[pl.ds(h, n - h)], land.at[pl.ds(2 * n + h, n - h)], r["up"])

    def ring_end(r, store):
        n, land = r["n"], r["land"]
        for name in ("raw_dn", "raw_up", "sum_dn", "sum_up"):
            r[name].wait_recv()
        mine = r["shard"](0)

        def one(i, carry):
            store(i, mine[i].astype(F32) + land[n + i].astype(F32) + land[2 * n + i].astype(F32))
            return carry

        lax.fori_loop(0, n, one, 0, unroll=2)

    order = (2, -1, 1, 0)
    gp = Group("x", "z", 0, ZFIRST)
    gq = Group("z", "x", ZFIRST, NB - ZFIRST)
    rings = {}
    for i, b in enumerate(order):
        for g in (gp, gq):
            shard = lambda a, g=g, b=b: g.local(a, b)
            land = inner.at[i, pl.ds(3 * g.lo, 3 * g.n)]
            rings[g, b] = ring_start(g.f, g.n, shard, land)
    wys = [
        copies.start(wg.at[pl.ds(4 * ((y + k) % NY), 4)], wy.at[k - 1], d)
        for k, d in enumerate(ypeers, 1)
    ]

    def keep(g, i):
        def store(j, v):
            summed[i, g.lo + j] = v.astype(BF)

        return store

    for i, b in enumerate(order):
        for g in (gp, gq):
            ring_forward(rings[g, b], half.at[i, pl.ds(g.lo, g.n)])
        if i == 1:
            for cp in wys:
                cp.wait_recv()
            for j in range(4):
                v = wg[4 * y + j].astype(F32)
                for k in range(NY - 1):
                    v = v + wy[k, j].astype(F32)
                ws[j] = v.astype(BF)
            wcs = [copies.start(ws.at[2 * q + 1 - core], wc.at[q], cpeer) for q in range(2)]
    second = {}
    for i, b in enumerate(order):
        for g in (gp, gq):
            ring_end(rings[g, b], keep(g, i))
    for cp in wcs:
        cp.wait_recv()
    for q in range(2):
        wm[q] = (ws[2 * q + core].astype(F32) + wc[q].astype(F32)).astype(BF)
    wzc = copies.start(wm.at[1 - zl], wz, zpeer)
    place = {2: 0, -2: 0, -1: 1, 1: 2, 0: 3}
    for g in (gp, gq):
        shard = lambda a, g=g: summed.at[place[a], pl.ds(g.lo, g.n)]
        second[g] = ring_start(g.s, g.n, shard, tail.at[pl.ds(3 * g.lo, 3 * g.n)])
    wzc.wait_recv()
    w1[...] = (wm[zl].astype(F32) + wz[...].astype(F32)).astype(BF)
    wxs = [copies.start(w1, wx.at[k], d) for k, d in enumerate(xs)]
    for g in (gp, gq):
        ring_forward(second[g], half.at[4, pl.ds(g.lo, g.n)])
    for cp in wxs:
        cp.wait_recv()
    v = w1[...].astype(F32)
    for k in range(NX - 1):
        v = v + wx[k].astype(F32)
    w2[...] = v.astype(BF)
    wvs = [copies.start(w2, wv.at[k], d) for k, d in enumerate(zs)]
    for g in (gp, gq):

        def final(j, v, g=g):
            s = lax.rsqrt(deg[pl.ds(g.lo + j, 1), :].astype(F32))
            out[g.lo + j] = (v * s).astype(BF)

        ring_end(second[g], final)
    for cp in wvs:
        cp.wait_recv()
    v = w2[...].astype(F32)
    for k in range(NZ - 1):
        v = v + wv[k].astype(F32)
    wout[...] = v
    copies.finish()


N_SCATTER = 2 * (4 * 6 + 6) + (NY - 1) + 2 + 1 + (NX - 1) + (NZ - 1)


def scatter_rows(part, degree, wg):
    vm = pl.BlockSpec(memory_space=pltpu.VMEM)
    f = wg.shape[2]
    return pl.pallas_call(
        scatter_kernel,
        name="scatter_rows",
        out_shape=(
            jax.ShapeDtypeStruct((NB, FS, BLK), BF),
            jax.ShapeDtypeStruct((FS, f), F32),
        ),
        in_specs=[vm] * 3,
        out_specs=(vm, vm),
        scratch_shapes=[
            pltpu.VMEM((4, 3 * NB, FS, BLK), BF),
            pltpu.VMEM((4, NB, FS, BLK), BF),
            pltpu.VMEM((5, NB, FS, BLK), BF),
            pltpu.VMEM((3 * NB, FS, BLK), BF),
            pltpu.VMEM((NY - 1, 4, FS, f), BF),
            pltpu.VMEM((4, FS, f), BF),
            pltpu.VMEM((2, FS, f), BF),
            pltpu.VMEM((2, FS, f), BF),
            pltpu.VMEM((FS, f), BF),
            pltpu.VMEM((FS, f), BF),
            pltpu.VMEM((NX - 1, FS, f), BF),
            pltpu.VMEM((FS, f), BF),
            pltpu.VMEM((NZ - 1, FS, f), BF),
            pltpu.SemaphoreType.DMA((N_SCATTER,)),
            pltpu.SemaphoreType.DMA((N_SCATTER,)),
        ],
        compiler_params=pltpu.CompilerParams(
            collective_id=2, has_side_effects=True, vmem_limit_bytes=32 << 20
        ),
    )(part, degree, wg)


def body(features, cotangent, weight, degree, tile_row, tile_col, tile_count, tile_weights):
    gathered, wt, cotx = gather_rows(features, degree, cotangent, weight)
    hidden = aggregate(gathered, degree, tile_col, tile_row, tile_count, tile_weights)
    activated, back, wg = dense(hidden, cotx, weight, wt, degree)
    part = spread(back, tile_col, tile_row, tile_count, tile_weights)
    input_grad, weight_grad = scatter_rows(part, degree, wg)
    return (activated, input_grad, weight_grad)


def solution(mesh):
    in_specs = (
        P("rows", "cols", None),
        P("rows", "cols", None),
        P(),
        P("rows", None),
        P("rows"),
        P("rows"),
        P("rows"),
        P("rows", None, None),
    )
    out_specs = (P("rows", "cols", None), P("rows", "cols", None), P("cols", None))
    return jax.shard_map(body, mesh=mesh, in_specs=in_specs, out_specs=out_specs, check_vma=False)
```

```python
import functools

import jax
import jax.numpy as jnp
from jax import lax
from jax.experimental import pallas as pl
from jax.experimental.pallas import tpu as pltpu
from jax.sharding import PartitionSpec as P

BF = jnp.bfloat16
F32 = jnp.float32
NB = 32
FS = 32
BLK = 128
NX = 4
NZ = 4
NR = NX * NZ
NY = 4
NC = 16
ZFIRST = 26
TB = 16
T = 256
DEAD = 1024


def rank_along(axis, step):
    r = lax.axis_index("rows")
    x, z = r // NZ, r % NZ
    if axis == "x":
        return ((x + step + NX) % NX) * NZ + z
    return x * NZ + (z + step + NZ) % NZ


def owner_at(first, a, second, b):
    r = lax.axis_index("rows")
    step = {first: a, second: b}
    return ((r // NZ + step["x"] + NX) % NX) * NZ + (r % NZ + step["z"] + NZ) % NZ


class Copies:
    def __init__(self, send, recv):
        self.send, self.recv, self.n, self.started = send, recv, 0, []

    def start(self, src, dst, device):
        k = self.n
        self.n += 1
        c = pltpu.make_async_remote_copy(
            src_ref=src,
            dst_ref=dst,
            send_sem=self.send.at[k],
            recv_sem=self.recv.at[k],
            device_id=device,
            device_id_type=pl.DeviceIdType.MESH,
        )
        c.start()
        self.started.append(c)
        return c

    def finish(self):
        for c in self.started:
            c.wait_send()


def greet(devices):
    barrier = pltpu.get_barrier_semaphore()
    for d in devices:
        pl.semaphore_signal(barrier, inc=1, device_id=d, device_id_type=pl.DeviceIdType.MESH)


def greeted(devices):
    pl.semaphore_wait(pltpu.get_barrier_semaphore(), len(devices))


def other_cols():
    c = lax.axis_index("cols")
    return [{"cols": (c + k) % NC} for k in range(1, NC)]


PERM, COLP, KEYP, ROW, COL, COLEND, ROWEND = range(7)


def tile_order(rowcol, count, idx_v):
    i32 = jnp.int32
    lane = lax.broadcasted_iota(i32, (1, T), 1)
    live = lane < count[0]
    row, col = rowcol[0], rowcol[1]
    key = jnp.where(live, row, DEAD)
    ckey = jnp.where(live, col, DEAD)

    def down(v):
        return jnp.broadcast_to(v, (8, T)).T[:, :1]

    def total(mask):
        return jnp.sum(mask.astype(i32), axis=0, keepdims=True)

    key_d, col_d, ckey_d = down(key), down(col), down(ckey)
    sub = lax.broadcasted_iota(i32, (T, T), 0)
    across = lax.broadcasted_iota(i32, (T, T), 1)
    pos = total((key_d < key) | ((key_d == key) & (sub < across)))
    here = down(pos) == across

    def sorted_(v_d):
        return jnp.sum(jnp.where(here, v_d, 0), axis=0, keepdims=True)

    def ends(v_d, n):
        b = lax.broadcasted_iota(i32, (T, n), 1)
        return jnp.where(total(v_d == b) > 0, total(v_d <= b) - 1, T)

    idx_v[pl.ds(PERM, 1), :T] = sorted_(sub)
    idx_v[pl.ds(COLP, 1), :T] = sorted_(col_d)
    idx_v[pl.ds(KEYP, 1), :T] = sorted_(key_d)
    idx_v[pl.ds(ROW, 1), :T] = row
    idx_v[pl.ds(COL, 1), :T] = ckey
    idx_v[pl.ds(COLEND, 1), :] = ends(ckey_d, NR * NB)
    idx_v[pl.ds(ROWEND, 1), :BLK] = ends(key_d, BLK)


def layer_kernel(
    feat, cot, w_h, deg_h, row_h, col_h, count, a_h,
    act, out, wout,
    fbuf, deg, w, wt, rowcol, a, idx_v, idx, gat, cotx, sums, hid, hx, act_s, back_s, back, runs, part, wg,
    inner, summed, half, tail, wy, ws, wc, wm, wz, w1, wx, w2, wv,
    send, recv, lsem,
):
    me = lax.axis_index("rows")
    c = lax.axis_index("cols")
    y, low = c // 4, c % 4
    zl, core = low // 2, low % 2
    devs = other_cols()
    ypeers = [{"cols": ((y + k) % NY) * 4 + low} for k in range(1, NY)]
    cpeer = {"cols": c + 1 - 2 * core}
    zpeer = {"cols": c + 2 - 4 * zl}
    xs = [{"rows": rank_along("x", k)} for k in range(1, NX)]
    zs = [{"rows": rank_along("z", k)} for k in range(1, NZ)]
    peers = devs + xs + zs
    greet(peers)
    loads = []

    def load(src, dst):
        cp = pltpu.make_async_copy(src, dst, lsem.at[len(loads)])
        cp.start()
        loads.append(cp)
        return cp

    l_feat = load(feat, fbuf)
    l_deg = load(deg_h, deg)
    l_idx = [load(row_h, rowcol.at[0]), load(col_h, rowcol.at[1])]
    l_w = load(w_h, w)
    l_cot = load(cot.at[pl.ds(2 * c, 2)], cotx.at[c])
    l_a = [load(a_h.at[pl.ds(i * T // 4, T // 4)], a.at[pl.ds(i * T // 4, T // 4)]) for i in range(4)]
    l_feat.wait()
    l_deg.wait()

    def scale_of(b):
        return lax.rsqrt(deg[pl.ds(b, 1), :].astype(F32))

    def scale_block(b, carry):
        gat[me * NB + b] = (fbuf[b].astype(F32) * scale_of(b)).astype(BF)
        return carry

    lax.fori_loop(0, NB, scale_block, 0, unroll=4)
    greeted(peers)
    copies = Copies(send, recv)

    class Gather:
        def __init__(self, first, second, lo, n, chunks):
            self.f, self.s, self.chunks = first, second, chunks
            self.size = n // chunks
            self.at = [lo + i * self.size for i in range(chunks)]
            h = chunks // 2
            self.up_order = list(range(chunks))
            self.dn_order = list(range(chunks))[::-1]
            self.up_half = self.up_order[:h]
            self.dn_half = self.dn_order[: chunks - h]
            self.a, self.b = {}, {}

        def push(self, a, b, i, axis, step):
            at = self.at[i]
            ds = pl.ds(owner_at(self.f, a, self.s, b) * NB + at, self.size)
            return copies.start(gat.at[ds], gat.at[ds], {"rows": rank_along(axis, step)})

        def first_start(self):
            for u, d in zip(self.up_order, self.dn_order):
                self.a[-1, u] = self.push(0, 0, u, self.f, 1)
                self.a[1, d] = self.push(0, 0, d, self.f, -1)

        def first_forward(self, j, then=None):
            for side, order, half in ((-1, self.up_order, self.up_half), (1, self.dn_order, self.dn_half)):
                i = order[j]
                self.a[side, i].wait_recv()
                if i in half:
                    self.a[2 * side, i] = self.push(side, 0, i, self.f, -side)
                if then:
                    then(side, i)

        def far(self, j, then):
            for side, half in ((-1, self.up_half), (1, self.dn_half)):
                if j < len(half):
                    self.a[2 * side, half[j]].wait_recv()
                    then(2 * side, half[j])

        def second_start(self, a, i):
            self.b[a, -1, i] = self.push(a, 0, i, self.s, 1)
            self.b[a, 1, i] = self.push(a, 0, i, self.s, -1)

        def second_forward(self, a, i):
            side = -1 if i in self.up_half else 1
            self.b[a, side, i].wait_recv()
            last.append(self.push(a, side, i, self.s, -side))
            last.append(self.b[a, -side, i])

    PC, QC = 2, 2
    last = []
    gp = Gather("z", "x", 0, ZFIRST, PC)
    gq = Gather("x", "z", ZFIRST, NB - ZFIRST, QC)
    gp.first_start()
    gq.first_start()
    for i in range(PC):
        gp.second_start(0, i)
    for k, dev in enumerate(devs, 1):
        last.append(copies.start(cot.at[pl.ds(2 * ((c + k) % NC), 2)], cotx.at[c], dev))
    for cp in l_idx:
        cp.wait()
    tile_order(rowcol, count, idx_v)
    l_s = load(idx_v, idx)
    l_w.wait()
    wt[...] = w[...].T
    for j in range(QC):
        gq.first_forward(j)
    for j in range(PC):
        gp.first_forward(j, gp.second_start)
    for i in range(QC):
        gq.second_start(0, i)
    for i in range(PC):
        gp.second_forward(0, i)
    for j in range(QC):
        gq.second_start(-1, gq.up_order[j])
        gq.second_start(1, gq.dn_order[j])
    for j in range((PC + 1) // 2):
        gp.far(j, gp.second_start)
    for i in range(PC):
        gp.second_forward(-1, i)
        gp.second_forward(1, PC - 1 - i)
    for i in range(QC):
        gq.second_forward(0, i)
    for j in range((QC + 1) // 2):
        gq.far(j, gq.second_start)
    for i in range(QC):
        gq.second_forward(-1, i)
        gq.second_forward(1, QC - 1 - i)
    for j in range((PC + 1) // 2):
        gp.second_forward(-2, gp.up_half[j])
        gp.second_forward(2, gp.dn_half[j])
    for j in range((QC + 1) // 2):
        gq.second_forward(-2, gq.up_half[j])
        gq.second_forward(2, gq.dn_half[j])
    for cp in last:
        cp.wait_recv()
    for cp in l_a + [l_s, l_cot]:
        cp.wait()

    sums[T] = jnp.zeros((FS, BLK), F32)

    def forward(i, run):
        for k in range(TB):
            p = i * TB + k
            m = lax.dot_general(
                gat[idx[COLP, p]], a[idx[PERM, p]], (((1,), (1,)), ((), ())), preferred_element_type=F32
            )
            same = idx[KEYP, p] == idx[KEYP, jnp.maximum(p - 1, 0)]
            run = jnp.where(same, run, 0.0) + m
            sums[p] = run
        return run

    lax.fori_loop(0, T // TB, forward, jnp.zeros((FS, BLK), F32))

    def finish_row(b, carry):
        hid[b] = (sums[idx[ROWEND, b]] * scale_of(b)).astype(BF)
        return carry

    lax.fori_loop(0, NB, finish_row, 0, unroll=4)

    arrivals = [
        copies.start(hid.at[pl.ds(2 * ((c + k) % NC), 2)], hx.at[c], dev)
        for k, dev in enumerate(devs, 1)
    ]
    hx[c] = hid[pl.ds(2 * c, 2)]
    runs[T] = jnp.zeros((FS, BLK), BF)
    for cp in arrivals:
        cp.wait_recv()

    def wide(ref):
        return jnp.concatenate([ref[:, b].reshape(NC * FS, BLK) for b in range(2)], axis=1)

    def narrow(ref, value):
        for b in range(2):
            ref[:, b] = value[:, b * BLK : (b + 1) * BLK].reshape(NC, FS, BLK)

    def to_owner(src, dst):
        got = [
            copies.start(src.at[(c + k) % NC], dst.at[pl.ds(2 * c, 2)], dev)
            for k, dev in enumerate(devs, 1)
        ]
        return got, load(src.at[c], dst.at[pl.ds(2 * c, 2)])

    x = wide(hx)
    pre = jnp.dot(wt[...], x, preferred_element_type=F32)
    sig = jax.nn.sigmoid(pre)
    slope = (wide(cotx).astype(F32) * sig * (1.0 + pre * (1.0 - sig))).astype(BF)
    s = jnp.concatenate([scale_of(2 * c + b) for b in range(2)], axis=1)
    narrow(back_s, (jnp.dot(w[...], slope, preferred_element_type=F32) * s).astype(BF))
    got_b, mine_b = to_owner(back_s, back)
    narrow(act_s, (pre * sig).astype(BF))
    got_a, mine_a = to_owner(act_s, act)
    wg[...] = (
        lax.dot_general(x, slope, (((1,), (1,)), ((), ())), preferred_element_type=F32)
        .astype(BF)
        .reshape(wg.shape)
    )
    wys = [
        copies.start(wg.at[pl.ds(4 * ((y + k) % NY), 4)], wy.at[k - 1], d)
        for k, d in enumerate(ypeers, 1)
    ]
    for cp in got_b:
        cp.wait_recv()
    mine_b.wait()

    def backward(i, run):
        for k in range(TB):
            t = i * TB + k
            m = jnp.dot(back[idx[ROW, t]], a[t], preferred_element_type=F32)
            same = idx[COL, t] == idx[COL, jnp.maximum(t - 1, 0)]
            run = jnp.where(same, run, 0.0) + m
            runs[t] = run.astype(BF)
        return run

    lax.fori_loop(0, T // TB, backward, jnp.zeros((FS, BLK), F32))

    def pick(i, carry):
        part[i] = runs[idx[COLEND, i]]
        return carry

    lax.fori_loop(0, NR * NB, pick, 0, unroll=8)

    class Shards:
        def __init__(self, first, second, lo, n):
            self.f, self.s, self.lo, self.n = first, second, lo, n

        def local(self, a, b):
            return part.at[pl.ds(owner_at(self.f, a, self.s, b) * NB + self.lo, self.n)]

    def ring_start(axis, n, shard, land):
        h = n // 2
        up, dn = {"rows": rank_along(axis, 1)}, {"rows": rank_along(axis, -1)}
        return {
            "n": n,
            "up": up,
            "dn": dn,
            "shard": shard,
            "land": land,
            "far_dn": copies.start(shard(-2).at[pl.ds(0, h)], land.at[pl.ds(0, h)], dn),
            "far_up": copies.start(shard(2).at[pl.ds(h, n - h)], land.at[pl.ds(h, n - h)], up),
            "raw_dn": copies.start(shard(-1).at[pl.ds(h, n - h)], land.at[pl.ds(n + h, n - h)], dn),
            "raw_up": copies.start(shard(1).at[pl.ds(0, h)], land.at[pl.ds(2 * n, h)], up),
        }

    def add_into(dst, a, b):
        def one(i, carry):
            dst[i] = (a[i].astype(F32) + b[i].astype(F32)).astype(BF)
            return carry

        lax.fori_loop(0, dst.shape[0], one, 0, unroll=2)

    def ring_forward(r, work):
        n, land = r["n"], r["land"]
        h = n // 2
        r["far_dn"].wait_recv()
        add_into(work.at[pl.ds(0, h)], land.at[pl.ds(0, h)], r["shard"](-1).at[pl.ds(0, h)])
        r["sum_dn"] = copies.start(work.at[pl.ds(0, h)], land.at[pl.ds(n, h)], r["dn"])
        r["far_up"].wait_recv()
        add_into(
            work.at[pl.ds(h, n - h)], land.at[pl.ds(h, n - h)], r["shard"](1).at[pl.ds(h, n - h)]
        )
        r["sum_up"] = copies.start(work.at[pl.ds(h, n - h)], land.at[pl.ds(2 * n + h, n - h)], r["up"])

    def ring_end(r, store):
        n, land = r["n"], r["land"]
        for name in ("raw_dn", "raw_up", "sum_dn", "sum_up"):
            r[name].wait_recv()
        mine = r["shard"](0)

        def one(i, carry):
            store(i, mine[i].astype(F32) + land[n + i].astype(F32) + land[2 * n + i].astype(F32))
            return carry

        lax.fori_loop(0, n, one, 0, unroll=2)

    order = (2, -1, 1, 0)
    gp = Shards("x", "z", 0, ZFIRST)
    gq = Shards("z", "x", ZFIRST, NB - ZFIRST)
    rings = {}
    for i, b in enumerate(order):
        for g in (gp, gq):
            shard = lambda a, g=g, b=b: g.local(a, b)
            land = inner.at[i, pl.ds(3 * g.lo, 3 * g.n)]
            rings[g, b] = ring_start(g.f, g.n, shard, land)

    def keep(g, i):
        def store(j, v):
            summed[i, g.lo + j] = v.astype(BF)

        return store

    for i, b in enumerate(order):
        for g in (gp, gq):
            ring_forward(rings[g, b], half.at[i, pl.ds(g.lo, g.n)])
        if i == 1:
            for cp in wys:
                cp.wait_recv()
            for j in range(4):
                v = wg[4 * y + j].astype(F32)
                for k in range(NY - 1):
                    v = v + wy[k, j].astype(F32)
                ws[j] = v.astype(BF)
            wcs = [copies.start(ws.at[2 * q + 1 - core], wc.at[q], cpeer) for q in range(2)]
    second = {}
    for i, b in enumerate(order):
        for g in (gp, gq):
            ring_end(rings[g, b], keep(g, i))
    for cp in wcs:
        cp.wait_recv()
    for q in range(2):
        wm[q] = (ws[2 * q + core].astype(F32) + wc[q].astype(F32)).astype(BF)
    wzc = copies.start(wm.at[1 - zl], wz, zpeer)
    place = {2: 0, -2: 0, -1: 1, 1: 2, 0: 3}
    for g in (gp, gq):
        shard = lambda a, g=g: summed.at[place[a], pl.ds(g.lo, g.n)]
        second[g] = ring_start(g.s, g.n, shard, tail.at[pl.ds(3 * g.lo, 3 * g.n)])
    wzc.wait_recv()
    w1[...] = (wm[zl].astype(F32) + wz[...].astype(F32)).astype(BF)
    wxs = [copies.start(w1, wx.at[k], d) for k, d in enumerate(xs)]
    for g in (gp, gq):
        ring_forward(second[g], half.at[4, pl.ds(g.lo, g.n)])
    for cp in wxs:
        cp.wait_recv()
    v = w1[...].astype(F32)
    for k in range(NX - 1):
        v = v + wx[k].astype(F32)
    w2[...] = v.astype(BF)
    wvs = [copies.start(w2, wv.at[k], d) for k, d in enumerate(zs)]
    for g in (gp, gq):

        def final(j, v, g=g):
            out[g.lo + j] = (v * scale_of(g.lo + j)).astype(BF)

        ring_end(second[g], final)
    for cp in wvs:
        cp.wait_recv()
    v = w2[...].astype(F32)
    for k in range(NZ - 1):
        v = v + wv[k].astype(F32)
    wout[...] = v
    for cp in got_a:
        cp.wait_recv()
    mine_a.wait()
    copies.finish()


N_COPIES = 2 * 2 * 15 + 4 * (NC - 1) + 2 * (4 * 6 + 6) + (NY - 1) + 2 + 1 + (NX - 1) + (NZ - 1)


def body(features, cotangent, weight, degree, tile_row, tile_col, tile_count, tile_weights):
    hb = pl.BlockSpec(memory_space=pl.ANY)
    vm = pl.BlockSpec(memory_space=pltpu.VMEM)
    sm = pl.BlockSpec(memory_space=pltpu.SMEM)
    f = weight.shape[1]
    shard = (FS, BLK)
    return pl.pallas_call(
        layer_kernel,
        name="layer",
        out_shape=(
            jax.ShapeDtypeStruct((NB,) + shard, BF),
            jax.ShapeDtypeStruct((NB,) + shard, BF),
            jax.ShapeDtypeStruct((FS, f), F32),
        ),
        in_specs=[hb, hb, hb, hb, hb, hb, sm, hb],
        out_specs=(hb, vm, vm),
        scratch_shapes=[
            pltpu.VMEM((NB,) + shard, BF),
            pltpu.VMEM((NB, BLK), jnp.int32),
            pltpu.VMEM(weight.shape, BF),
            pltpu.VMEM(weight.shape, BF),
            pltpu.VMEM((2, 1, T), jnp.int32),
            pltpu.VMEM((T, BLK, BLK), BF),
            pltpu.VMEM((8, NR * NB), jnp.int32),
            pltpu.SMEM((8, NR * NB), jnp.int32),
            pltpu.VMEM((NR * NB,) + shard, BF),
            pltpu.VMEM((NC, 2) + shard, BF),
            pltpu.VMEM((T + 1,) + shard, F32),
            pltpu.VMEM((NB,) + shard, BF),
            pltpu.VMEM((NC, 2) + shard, BF),
            pltpu.VMEM((NC, 2) + shard, BF),
            pltpu.VMEM((NC, 2) + shard, BF),
            pltpu.VMEM((NB,) + shard, BF),
            pltpu.VMEM((T + 1,) + shard, BF),
            pltpu.VMEM((NR * NB,) + shard, BF),
            pltpu.VMEM((NC, FS, f), BF),
            pltpu.VMEM((4, 3 * NB) + shard, BF),
            pltpu.VMEM((4, NB) + shard, BF),
            pltpu.VMEM((5, NB) + shard, BF),
            pltpu.VMEM((3 * NB,) + shard, BF),
            pltpu.VMEM((NY - 1, 4, FS, f), BF),
            pltpu.VMEM((4, FS, f), BF),
            pltpu.VMEM((2, FS, f), BF),
            pltpu.VMEM((2, FS, f), BF),
            pltpu.VMEM((FS, f), BF),
            pltpu.VMEM((FS, f), BF),
            pltpu.VMEM((NX - 1, FS, f), BF),
            pltpu.VMEM((FS, f), BF),
            pltpu.VMEM((NZ - 1, FS, f), BF),
            pltpu.SemaphoreType.DMA((N_COPIES,)),
            pltpu.SemaphoreType.DMA((N_COPIES,)),
            pltpu.SemaphoreType.DMA((16,)),
        ],
        compiler_params=pltpu.CompilerParams(
            collective_id=0, has_side_effects=True, vmem_limit_bytes=60 << 20
        ),
    )(
        features,
        cotangent,
        weight,
        degree,
        tile_row.reshape(1, T),
        tile_col.reshape(1, T),
        tile_count,
        tile_weights,
    )


def solution(mesh):
    in_specs = (
        P("rows", "cols", None),
        P("rows", "cols", None),
        P(),
        P("rows", None),
        P("rows"),
        P("rows"),
        P("rows"),
        P("rows", None, None),
    )
    out_specs = (P("rows", "cols", None), P("rows", "cols", None), P("cols", None))
    return jax.shard_map(body, mesh=mesh, in_specs=in_specs, out_specs=out_specs, check_vma=False)
```

```python
import functools

import jax
import jax.numpy as jnp
from jax import lax
from jax.experimental import pallas as pl
from jax.experimental.pallas import tpu as pltpu
from jax.sharding import PartitionSpec as P

BF = jnp.bfloat16
F32 = jnp.float32
NB = 32
FS = 32
BLK = 128
NX = 4
NZ = 4
NR = NX * NZ
NY = 4
NC = 16
ZFIRST = 26
XFIRST = 26
TC = 64
TB = 16
T = 256
DEAD = 1024


def rank_along(axis, step):
    r = lax.axis_index("rows")
    x, z = r // NZ, r % NZ
    if axis == "x":
        return ((x + step + NX) % NX) * NZ + z
    return x * NZ + (z + step + NZ) % NZ


def owner_at(first, a, second, b):
    r = lax.axis_index("rows")
    step = {first: a, second: b}
    return ((r // NZ + step["x"] + NX) % NX) * NZ + (r % NZ + step["z"] + NZ) % NZ


class Copies:
    def __init__(self, send, recv):
        self.send, self.recv, self.n, self.started = send, recv, 0, []

    def start(self, src, dst, device):
        k = self.n
        self.n += 1
        c = pltpu.make_async_remote_copy(
            src_ref=src,
            dst_ref=dst,
            send_sem=self.send.at[k],
            recv_sem=self.recv.at[k],
            device_id=device,
            device_id_type=pl.DeviceIdType.MESH,
        )
        c.start()
        self.started.append(c)
        return c

    def finish(self):
        for c in self.started:
            c.wait_send()


def greet(devices):
    barrier = pltpu.get_barrier_semaphore()
    for d in devices:
        pl.semaphore_signal(barrier, inc=1, device_id=d, device_id_type=pl.DeviceIdType.MESH)


def greeted(devices):
    pl.semaphore_wait(pltpu.get_barrier_semaphore(), len(devices))


def other_cols():
    c = lax.axis_index("cols")
    y, z, core = c // 4, (c // 2) % 2, c % 2
    found = []
    for dy in (2, 1, 3, 0):
        for dz in (1, 0):
            for dc in (1, 0):
                if (dy, dz, dc) != (0, 0, 0):
                    k = ((y + dy) % NY) * 4 + (z + dz - 2 * z * dz) * 2 + core + dc - 2 * core * dc
                    found.append((k, {"cols": k}))
    return found


PERM, COLP, KEYP, ROW, COL, COLEND, ROWEND = range(7)


def tile_order(rowcol, count, idx_v):
    i32 = jnp.int32
    lane = lax.broadcasted_iota(i32, (1, T), 1)
    live = lane < count[0]
    row, col = rowcol[0], rowcol[1]
    key = jnp.where(live, row, DEAD)
    ckey = jnp.where(live, col, DEAD)

    def down(v):
        return jnp.broadcast_to(v, (8, T)).T[:, :1]

    def total(mask):
        return jnp.sum(mask.astype(i32), axis=0, keepdims=True)

    key_d, col_d, ckey_d = down(key), down(col), down(ckey)
    sub = lax.broadcasted_iota(i32, (T, T), 0)
    across = lax.broadcasted_iota(i32, (T, T), 1)
    pos = total((key_d < key) | ((key_d == key) & (sub < across)))
    here = down(pos) == across

    def sorted_(v_d):
        return jnp.sum(jnp.where(here, v_d, 0), axis=0, keepdims=True)

    def ends(v_d, n):
        b = lax.broadcasted_iota(i32, (T, n), 1)
        return jnp.where(total(v_d == b) > 0, total(v_d <= b) - 1, T)

    idx_v[pl.ds(PERM, 1), :T] = sorted_(sub)
    idx_v[pl.ds(COLP, 1), :T] = sorted_(col_d)
    idx_v[pl.ds(KEYP, 1), :T] = sorted_(key_d)
    idx_v[pl.ds(ROW, 1), :T] = row
    idx_v[pl.ds(COL, 1), :T] = ckey
    idx_v[pl.ds(COLEND, 1), :] = ends(ckey_d, NR * NB)
    idx_v[pl.ds(ROWEND, 1), :BLK] = ends(key_d, BLK)


def layer_kernel(
    feat, cot, w_h, deg_h, row_h, col_h, count, a_h,
    act, out, wout,
    fbuf, deg, w, wt, rowcol, a, at, idx_v, idx, gat, cotx, sums, hid, hx, act_s, back_s, back, runs, part, wg,
    inner, summed, half, tail, wy, ws, wc, wm, wz, w1, wx, w2, wv,
    send, recv, lsem,
):
    me = lax.axis_index("rows")
    c = lax.axis_index("cols")
    y, low = c // 4, c % 4
    zl, core = low // 2, low % 2
    devs = other_cols()
    ypeers = [{"cols": ((y + k) % NY) * 4 + low} for k in range(1, NY)]
    cpeer = {"cols": c + 1 - 2 * core}
    zpeer = {"cols": c + 2 - 4 * zl}
    xs = [{"rows": rank_along("x", k)} for k in range(1, NX)]
    zs = [{"rows": rank_along("z", k)} for k in range(1, NZ)]
    peers = [d for _, d in devs] + xs + zs
    greet(peers)
    loads = []

    def load(src, dst):
        cp = pltpu.make_async_copy(src, dst, lsem.at[len(loads)])
        cp.start()
        loads.append(cp)
        return cp

    l_feat = load(feat, fbuf)
    l_deg = load(deg_h, deg)
    l_idx = [load(row_h, rowcol.at[0]), load(col_h, rowcol.at[1])]
    l_w = load(w_h, w)
    l_cot = load(cot.at[pl.ds(2 * c, 2)], cotx.at[c])
    l_a = [load(a_h.at[pl.ds(i * T // 4, T // 4)], a.at[pl.ds(i * T // 4, T // 4)]) for i in range(4)]
    l_feat.wait()
    l_deg.wait()

    def scale_of(b):
        return lax.rsqrt(deg[pl.ds(b, 1), :].astype(F32))

    def scale_block(b, carry):
        gat[me * NB + b] = (fbuf[b].astype(F32) * scale_of(b)).astype(BF)
        return carry

    lax.fori_loop(0, NB, scale_block, 0, unroll=4)
    greeted(peers)
    copies = Copies(send, recv)

    class Gather:
        def __init__(self, first, second, lo, n, chunks):
            self.f, self.s, self.chunks = first, second, chunks
            self.size = n // chunks
            self.at = [lo + i * self.size for i in range(chunks)]
            h = chunks // 2
            self.up_order = list(range(chunks))
            self.dn_order = list(range(chunks))[::-1]
            self.up_half = self.up_order[:h]
            self.dn_half = self.dn_order[: chunks - h]
            self.a, self.b = {}, {}

        def push(self, a, b, i, axis, step):
            at = self.at[i]
            ds = pl.ds(owner_at(self.f, a, self.s, b) * NB + at, self.size)
            return copies.start(gat.at[ds], gat.at[ds], {"rows": rank_along(axis, step)})

        def first_start(self):
            for u, d in zip(self.up_order, self.dn_order):
                self.a[-1, u] = self.push(0, 0, u, self.f, 1)
                self.a[1, d] = self.push(0, 0, d, self.f, -1)

        def first_forward(self, j, then=None):
            for side, order, half in ((-1, self.up_order, self.up_half), (1, self.dn_order, self.dn_half)):
                i = order[j]
                self.a[side, i].wait_recv()
                if i in half:
                    self.a[2 * side, i] = self.push(side, 0, i, self.f, -side)
                if then:
                    then(side, i)

        def far(self, j, then):
            for side, half in ((-1, self.up_half), (1, self.dn_half)):
                if j < len(half):
                    self.a[2 * side, half[j]].wait_recv()
                    then(2 * side, half[j])

        def second_start(self, a, i):
            self.b[a, -1, i] = self.push(a, 0, i, self.s, 1)
            self.b[a, 1, i] = self.push(a, 0, i, self.s, -1)

        def second_forward(self, a, i):
            side = -1 if i in self.up_half else 1
            self.b[a, side, i].wait_recv()
            last.append(self.push(a, side, i, self.s, -side))
            last.append(self.b[a, -side, i])

    PC, QC = 2, 2
    last = []
    gp = Gather("z", "x", 0, ZFIRST, PC)
    gq = Gather("x", "z", ZFIRST, NB - ZFIRST, QC)
    gp.first_start()
    gq.first_start()
    for i in range(PC):
        gp.second_start(0, i)
    for k, dev in devs:
        last.append(copies.start(cot.at[pl.ds(2 * k, 2)], cotx.at[c], dev))
    for cp in l_idx:
        cp.wait()
    tile_order(rowcol, count, idx_v)
    l_s = load(idx_v, idx)
    l_w.wait()
    wt[...] = w[...].T

    def turn(q):
        l_a[q].wait()

        def some(i, carry):
            for k in range(4):
                t = q * TC + i * 4 + k
                at[t] = a[t].T
            return carry

        lax.fori_loop(0, TC // 4, some, 0)

    for j in range(QC):
        gq.first_forward(j)
    turn(0)
    for j in range(PC):
        gp.first_forward(j, gp.second_start)
    for i in range(QC):
        gq.second_start(0, i)
    for i in range(PC):
        gp.second_forward(0, i)
    for j in range(QC):
        gq.second_start(-1, gq.up_order[j])
        gq.second_start(1, gq.dn_order[j])
    turn(1)
    for j in range((PC + 1) // 2):
        gp.far(j, gp.second_start)
    turn(2)
    for i in range(PC):
        gp.second_forward(-1, i)
        gp.second_forward(1, PC - 1 - i)
    turn(3)
    for i in range(QC):
        gq.second_forward(0, i)
    for j in range((QC + 1) // 2):
        gq.far(j, gq.second_start)
    for i in range(QC):
        gq.second_forward(-1, i)
        gq.second_forward(1, QC - 1 - i)
    for j in range((PC + 1) // 2):
        gp.second_forward(-2, gp.up_half[j])
        gp.second_forward(2, gp.dn_half[j])
    for j in range((QC + 1) // 2):
        gq.second_forward(-2, gq.up_half[j])
        gq.second_forward(2, gq.dn_half[j])
    for cp in last:
        cp.wait_recv()
    for cp in [l_s, l_cot]:
        cp.wait()

    sums[T] = jnp.zeros((FS, BLK), F32)

    def forward(i, run):
        for k in range(TB):
            p = i * TB + k
            m = lax.dot_general(
                gat[idx[COLP, p]], at[idx[PERM, p]], (((1,), (0,)), ((), ())), preferred_element_type=F32
            )
            same = idx[KEYP, p] == idx[KEYP, jnp.maximum(p - 1, 0)]
            run = jnp.where(same, run, 0.0) + m
            sums[p] = run
        return run

    lax.fori_loop(0, T // TB, forward, jnp.zeros((FS, BLK), F32))

    def finish_row(b, carry):
        hid[b] = (sums[idx[ROWEND, b]] * scale_of(b)).astype(BF)
        return carry

    lax.fori_loop(0, NB, finish_row, 0, unroll=4)

    arrivals = [
        copies.start(hid.at[pl.ds(2 * k, 2)], hx.at[c], dev)
        for k, dev in devs
    ]
    hx[c] = hid[pl.ds(2 * c, 2)]
    runs[T] = jnp.zeros((FS, BLK), BF)
    for cp in arrivals:
        cp.wait_recv()

    def wide(ref):
        return jnp.concatenate([ref[:, b].reshape(NC * FS, BLK) for b in range(2)], axis=1)

    def narrow(ref, value):
        for b in range(2):
            ref[:, b] = value[:, b * BLK : (b + 1) * BLK].reshape(NC, FS, BLK)

    def to_owner(src, dst):
        got = [
            copies.start(src.at[k], dst.at[pl.ds(2 * c, 2)], dev)
            for k, dev in devs
        ]
        return got, load(src.at[c], dst.at[pl.ds(2 * c, 2)])

    x = wide(hx)
    pre = jnp.dot(wt[...], x, preferred_element_type=F32)
    sig = jax.nn.sigmoid(pre)
    slope = (wide(cotx).astype(F32) * sig * (1.0 + pre * (1.0 - sig))).astype(BF)
    s = jnp.concatenate([scale_of(2 * c + b) for b in range(2)], axis=1)
    narrow(back_s, (jnp.dot(w[...], slope, preferred_element_type=F32) * s).astype(BF))
    got_b, mine_b = to_owner(back_s, back)
    narrow(act_s, (pre * sig).astype(BF))
    wg[...] = (
        lax.dot_general(x, slope, (((1,), (1,)), ((), ())), preferred_element_type=F32)
        .astype(BF)
        .reshape(wg.shape)
    )
    for cp in got_b:
        cp.wait_recv()
    mine_b.wait()

    def backward(i, run):
        for k in range(TB):
            t = i * TB + k
            m = jnp.dot(back[idx[ROW, t]], a[t], preferred_element_type=F32)
            same = idx[COL, t] == idx[COL, jnp.maximum(t - 1, 0)]
            run = jnp.where(same, run, 0.0) + m
            runs[t] = run.astype(BF)
        return run

    lax.fori_loop(0, T // TB, backward, jnp.zeros((FS, BLK), F32))

    def local(first, a, second, b, lo, n):
        return part.at[pl.ds(owner_at(first, a, second, b) * NB + lo, n)]

    def add_into(dst, p, q):
        def one(i, carry):
            dst[i] = (p[i].astype(F32) + q[i].astype(F32)).astype(BF)
            return carry

        lax.fori_loop(0, dst.shape[0], one, 0, unroll=2)

    class Ring:
        def __init__(self, axis, n, shard, land, work):
            self.n, self.h, self.shard, self.land, self.work = n, n // 2, shard, land, work
            self.up, self.dn = {"rows": rank_along(axis, 1)}, {"rows": rank_along(axis, -1)}
            self.got = []

        def far(self):
            n, h = self.n, self.h
            self.far_dn = copies.start(self.shard(-2).at[pl.ds(0, h)], self.land.at[pl.ds(0, h)], self.dn)
            self.far_up = copies.start(
                self.shard(2).at[pl.ds(h, n - h)], self.land.at[pl.ds(h, n - h)], self.up
            )

        def raw_dn(self):
            n, h = self.n, self.h
            self.got.append(
                copies.start(self.shard(-1).at[pl.ds(h, n - h)], self.land.at[pl.ds(n + h, n - h)], self.dn)
            )

        def raw_up(self):
            n, h = self.n, self.h
            self.got.append(
                copies.start(self.shard(1).at[pl.ds(0, h)], self.land.at[pl.ds(2 * n, h)], self.up)
            )

        def start(self):
            self.far()
            self.raw_dn()
            self.raw_up()

        def forward(self):
            n, h = self.n, self.h
            lo, hi = pl.ds(0, h), pl.ds(h, n - h)
            self.far_dn.wait_recv()
            add_into(self.work.at[lo], self.land.at[lo], self.shard(-1).at[lo])
            self.got.append(copies.start(self.work.at[lo], self.land.at[pl.ds(n, h)], self.dn))
            self.far_up.wait_recv()
            add_into(self.work.at[hi], self.land.at[hi], self.shard(1).at[hi])
            self.got.append(copies.start(self.work.at[hi], self.land.at[pl.ds(2 * n + h, n - h)], self.up))

        def end(self, store):
            n, land = self.n, self.land
            for cp in self.got:
                cp.wait_recv()
            mine = self.shard(0)

            def one(i, carry):
                store(i, mine[i].astype(F32) + land[n + i].astype(F32) + land[2 * n + i].astype(F32))
                return carry

            lax.fori_loop(0, n, one, 0, unroll=2)

    slot = {2: 0, -2: 0, -1: 1, 1: 2, 0: 3}

    def first_rings(first, second, lo, n):
        return {
            b: Ring(
                first,
                n,
                lambda a, b=b: local(first, a, second, b, lo, n),
                inner.at[slot[b], pl.ds(3 * lo, 3 * n)],
                half.at[slot[b], pl.ds(lo, n)],
            )
            for b in (2, -1, 1, 0)
        }

    def second_ring(second, lo, n):
        return Ring(
            second,
            n,
            lambda a: summed.at[slot[a], pl.ds(lo, n)],
            tail.at[pl.ds(3 * lo, 3 * n)],
            half.at[4, pl.ds(lo, n)],
        )

    def keep(b, lo):
        def store(j, v):
            summed[slot[b], lo + j] = v.astype(BF)

        return store

    def final(lo):
        def store(j, v):
            out[lo + j] = (v * scale_of(lo + j)).astype(BF)

        return store

    PN, QN = XFIRST, NB - XFIRST
    p1, p2 = first_rings("x", "z", 0, PN), second_ring("z", 0, PN)
    q1, q2 = first_rings("z", "x", PN, QN), second_ring("x", PN, QN)

    def pick(dx, dz, lo, n):
        first = owner_at("x", dx, "z", dz) * NB + lo

        def one(i, carry):
            part[first + i] = runs[idx[COLEND, first + i]]
            return carry

        lax.fori_loop(0, n, one, 0, unroll=True)

    away = (2, -1, 1, 0)
    for dx in away:
        pick(dx, 2, 0, PN)
    p1[2].start()
    for dz in away:
        for dx in away:
            pick(dx, dz, PN, QN)
    for b in away:
        q1[b].start()
    for dx in away:
        pick(dx, -1, 0, PN)
    p1[-1].start()
    for dz in (1, 0):
        for dx in away:
            pick(dx, dz, 0, PN)
    got_a, mine_a = to_owner(act_s, act)
    wys = [
        copies.start(wg.at[pl.ds(4 * ((y + k) % NY), 4)], wy.at[k - 1], d)
        for k, d in enumerate(ypeers, 1)
    ]
    p1[2].forward()
    p1[1].start()
    q1[2].forward()
    p1[2].end(keep(2, 0))
    p2.far()
    p1[-1].forward()
    p1[0].start()
    q1[-1].forward()
    q1[1].forward()
    q1[0].forward()
    for cp in wys:
        cp.wait_recv()
    for j in range(4):
        v = wg[4 * y + j].astype(F32)
        for k in range(NY - 1):
            v = v + wy[k, j].astype(F32)
        ws[j] = v.astype(BF)
    wcs = [copies.start(ws.at[2 * q + 1 - core], wc.at[q], cpeer) for q in range(2)]
    p1[-1].end(keep(-1, 0))
    p2.raw_dn()
    p1[1].forward()
    q1[2].end(keep(2, PN))
    q2.far()
    q1[-1].end(keep(-1, PN))
    q2.raw_dn()
    q1[1].end(keep(1, PN))
    q2.raw_up()
    for cp in wcs:
        cp.wait_recv()
    for q in range(2):
        wm[q] = (ws[2 * q + core].astype(F32) + wc[q].astype(F32)).astype(BF)
    wzc = copies.start(wm.at[1 - zl], wz, zpeer)
    q1[0].end(keep(0, PN))
    p1[1].end(keep(1, 0))
    p2.raw_up()
    p2.forward()
    q2.forward()
    p1[0].forward()
    wzc.wait_recv()
    w1[...] = (wm[zl].astype(F32) + wz[...].astype(F32)).astype(BF)
    wxs = [copies.start(w1, wx.at[k], d) for k, d in enumerate(xs)]
    q2.end(final(PN))
    for cp in wxs:
        cp.wait_recv()
    v = w1[...].astype(F32)
    for k in range(NX - 1):
        v = v + wx[k].astype(F32)
    w2[...] = v.astype(BF)
    wvs = [copies.start(w2, wv.at[k], d) for k, d in enumerate(zs)]
    p1[0].end(keep(0, 0))
    p2.end(final(0))
    for cp in wvs:
        cp.wait_recv()
    v = w2[...].astype(F32)
    for k in range(NZ - 1):
        v = v + wv[k].astype(F32)
    wout[...] = v
    for cp in got_a:
        cp.wait_recv()
    mine_a.wait()
    copies.finish()


def hand_over_kernel(a_in, b_in, c_in, a_out, b_out, c_out, sem):
    moves = [
        pltpu.make_async_copy(src, dst, sem.at[i])
        for i, (src, dst) in enumerate(((a_in, a_out), (b_in, b_out), (c_in, c_out)))
    ]
    for m in moves:
        m.start()
    for m in moves:
        m.wait()


def hand_over(results):
    vm = pl.BlockSpec(memory_space=pltpu.VMEM)
    hb = pl.BlockSpec(memory_space=pl.ANY)
    return pl.pallas_call(
        hand_over_kernel,
        name="hand_over",
        out_shape=tuple(jax.ShapeDtypeStruct(r.shape, r.dtype) for r in results),
        in_specs=[vm] * 3,
        out_specs=(hb,) * 3,
        scratch_shapes=[pltpu.SemaphoreType.DMA((3,))],
        compiler_params=pltpu.CompilerParams(vmem_limit_bytes=60 << 20),
    )(*results)


N_COPIES = 2 * 2 * 15 + 4 * (NC - 1) + 2 * (4 * 6 + 6) + (NY - 1) + 2 + 1 + (NX - 1) + (NZ - 1)


def body(features, cotangent, weight, degree, tile_row, tile_col, tile_count, tile_weights):
    hb = pl.BlockSpec(memory_space=pl.ANY)
    vm = pl.BlockSpec(memory_space=pltpu.VMEM)
    sm = pl.BlockSpec(memory_space=pltpu.SMEM)
    f = weight.shape[1]
    shard = (FS, BLK)
    results = pl.pallas_call(
        layer_kernel,
        name="layer",
        out_shape=(
            jax.ShapeDtypeStruct((NB,) + shard, BF),
            jax.ShapeDtypeStruct((NB,) + shard, BF),
            jax.ShapeDtypeStruct((FS, f), F32),
        ),
        in_specs=[hb, hb, hb, hb, hb, hb, sm, hb],
        out_specs=(hb, vm, vm),
        scratch_shapes=[
            pltpu.VMEM((NB,) + shard, BF),
            pltpu.VMEM((NB, BLK), jnp.int32),
            pltpu.VMEM(weight.shape, BF),
            pltpu.VMEM(weight.shape, BF),
            pltpu.VMEM((2, 1, T), jnp.int32),
            pltpu.VMEM((T, BLK, BLK), BF),
            pltpu.VMEM((T, BLK, BLK), BF),
            pltpu.VMEM((8, NR * NB), jnp.int32),
            pltpu.SMEM((8, NR * NB), jnp.int32),
            pltpu.VMEM((NR * NB,) + shard, BF),
            pltpu.VMEM((NC, 2) + shard, BF),
            pltpu.VMEM((T + 1,) + shard, F32),
            pltpu.VMEM((NB,) + shard, BF),
            pltpu.VMEM((NC, 2) + shard, BF),
            pltpu.VMEM((NC, 2) + shard, BF),
            pltpu.VMEM((NC, 2) + shard, BF),
            pltpu.VMEM((NB,) + shard, BF),
            pltpu.VMEM((T + 1,) + shard, BF),
            pltpu.VMEM((NR * NB,) + shard, BF),
            pltpu.VMEM((NC, FS, f), BF),
            pltpu.VMEM((4, 3 * NB) + shard, BF),
            pltpu.VMEM((4, NB) + shard, BF),
            pltpu.VMEM((5, NB) + shard, BF),
            pltpu.VMEM((3 * NB,) + shard, BF),
            pltpu.VMEM((NY - 1, 4, FS, f), BF),
            pltpu.VMEM((4, FS, f), BF),
            pltpu.VMEM((2, FS, f), BF),
            pltpu.VMEM((2, FS, f), BF),
            pltpu.VMEM((FS, f), BF),
            pltpu.VMEM((FS, f), BF),
            pltpu.VMEM((NX - 1, FS, f), BF),
            pltpu.VMEM((FS, f), BF),
            pltpu.VMEM((NZ - 1, FS, f), BF),
            pltpu.SemaphoreType.DMA((N_COPIES,)),
            pltpu.SemaphoreType.DMA((N_COPIES,)),
            pltpu.SemaphoreType.DMA((16,)),
        ],
        compiler_params=pltpu.CompilerParams(
            collective_id=0, has_side_effects=True, vmem_limit_bytes=60 << 20
        ),
    )(
        features,
        cotangent,
        weight,
        degree,
        tile_row.reshape(1, T),
        tile_col.reshape(1, T),
        tile_count,
        tile_weights,
    )
    return hand_over(results)


def solution(mesh):
    in_specs = (
        P("rows", "cols", None),
        P("rows", "cols", None),
        P(),
        P("rows", None),
        P("rows"),
        P("rows"),
        P("rows"),
        P("rows", None, None),
    )
    out_specs = (P("rows", "cols", None), P("rows", "cols", None), P("cols", None))
    return jax.shard_map(body, mesh=mesh, in_specs=in_specs, out_specs=out_specs, check_vma=False)
```

```python
import functools

import jax
import jax.numpy as jnp
from jax import lax
from jax.experimental import pallas as pl
from jax.experimental.pallas import tpu as pltpu
from jax.sharding import PartitionSpec as P

BF = jnp.bfloat16
F32 = jnp.float32
NB = 32
FS = 32
BLK = 128
NX = 4
NZ = 4
NR = NX * NZ
NY = 4
NC = 16
ZFIRST = 26
XFIRST = 26
TC = 64
TB = 64
T = 256
DEAD = 1024


def rank_along(axis, step):
    r = lax.axis_index("rows")
    x, z = r // NZ, r % NZ
    if axis == "x":
        return ((x + step + NX) % NX) * NZ + z
    return x * NZ + (z + step + NZ) % NZ


def owner_at(first, a, second, b):
    r = lax.axis_index("rows")
    step = {first: a, second: b}
    return ((r // NZ + step["x"] + NX) % NX) * NZ + (r % NZ + step["z"] + NZ) % NZ


class Copies:
    def __init__(self, send, recv):
        self.send, self.recv, self.n, self.started = send, recv, 0, []

    def start(self, src, dst, device):
        k = self.n
        self.n += 1
        c = pltpu.make_async_remote_copy(
            src_ref=src,
            dst_ref=dst,
            send_sem=self.send.at[k],
            recv_sem=self.recv.at[k],
            device_id=device,
            device_id_type=pl.DeviceIdType.MESH,
        )
        c.start()
        self.started.append(c)
        return c

    def finish(self):
        for c in self.started:
            c.wait_send()


def greet(devices):
    barrier = pltpu.get_barrier_semaphore()
    for d in devices:
        pl.semaphore_signal(barrier, inc=1, device_id=d, device_id_type=pl.DeviceIdType.MESH)


def greeted(devices):
    pl.semaphore_wait(pltpu.get_barrier_semaphore(), len(devices))


def other_cols():
    c = lax.axis_index("cols")
    y, z, core = c // 4, (c // 2) % 2, c % 2
    found = []
    for dy in (2, 1, 3, 0):
        for dz in (1, 0):
            for dc in (1, 0):
                if (dy, dz, dc) != (0, 0, 0):
                    k = ((y + dy) % NY) * 4 + (z + dz - 2 * z * dz) * 2 + core + dc - 2 * core * dc
                    found.append((k, {"cols": k}))
    return found


PERM, COLP, KEYP, ROW, COL, COLEND, ROWEND = range(7)


def tile_order(rowcol, count, idx_v):
    i32 = jnp.int32
    lane = lax.broadcasted_iota(i32, (1, T), 1)
    live = lane < count[0]
    row, col = rowcol[0], rowcol[1]
    key = jnp.where(live, row, DEAD)
    ckey = jnp.where(live, col, DEAD)

    def down(v):
        return jnp.broadcast_to(v, (8, T)).T[:, :1]

    def total(mask):
        return jnp.sum(mask.astype(i32), axis=0, keepdims=True)

    key_d, col_d, ckey_d = down(key), down(col), down(ckey)
    sub = lax.broadcasted_iota(i32, (T, T), 0)
    across = lax.broadcasted_iota(i32, (T, T), 1)
    pos = total((key_d < key) | ((key_d == key) & (sub < across)))
    here = down(pos) == across

    def sorted_(v_d):
        return jnp.sum(jnp.where(here, v_d, 0), axis=0, keepdims=True)

    def ends(v_d, n):
        b = lax.broadcasted_iota(i32, (T, n), 1)
        return jnp.where(total(v_d == b) > 0, total(v_d <= b) - 1, T)

    idx_v[pl.ds(PERM, 1), :T] = sorted_(sub)
    idx_v[pl.ds(COLP, 1), :T] = sorted_(col_d)
    idx_v[pl.ds(KEYP, 1), :T] = sorted_(key_d)
    idx_v[pl.ds(ROW, 1), :T] = row
    idx_v[pl.ds(COL, 1), :T] = ckey
    idx_v[pl.ds(COLEND, 1), :] = ends(ckey_d, NR * NB)
    idx_v[pl.ds(ROWEND, 1), :BLK] = ends(key_d, BLK)


def layer_kernel(
    feat, cot, w_h, deg_h, row_h, col_h, count, a_h,
    act, out, wout,
    fbuf, deg, w, wt, rowcol, a, at, idx_v, idx, gat, cotx, sums, hid, hx, act_s, back_s, back, runs, part, wg,
    inner, summed, half, tail, wy, ws, wc, wm, wz, w1, wx, w2, wv,
    send, recv, lsem,
):
    me = lax.axis_index("rows")
    c = lax.axis_index("cols")
    y, low = c // 4, c % 4
    zl, core = low // 2, low % 2
    devs = other_cols()
    ypeers = [{"cols": ((y + k) % NY) * 4 + low} for k in range(1, NY)]
    cpeer = {"cols": c + 1 - 2 * core}
    zpeer = {"cols": c + 2 - 4 * zl}
    xs = [{"rows": rank_along("x", k)} for k in range(1, NX)]
    zs = [{"rows": rank_along("z", k)} for k in range(1, NZ)]
    peers = [d for _, d in devs] + xs + zs
    greet(peers)
    loads = []

    def load(src, dst):
        cp = pltpu.make_async_copy(src, dst, lsem.at[len(loads)])
        cp.start()
        loads.append(cp)
        return cp

    l_feat = load(feat, fbuf)
    l_deg = load(deg_h, deg)
    l_idx = [load(row_h, rowcol.at[0]), load(col_h, rowcol.at[1])]
    l_w = load(w_h, w)
    l_cot = load(cot.at[pl.ds(2 * c, 2)], cotx.at[c])
    l_a = [load(a_h.at[pl.ds(i * T // 4, T // 4)], a.at[pl.ds(i * T // 4, T // 4)]) for i in range(4)]
    l_feat.wait()
    l_deg.wait()

    def scale_of(b):
        return lax.rsqrt(deg[pl.ds(b, 1), :].astype(F32))

    def scale_block(b, carry):
        gat[me * NB + b] = (fbuf[b].astype(F32) * scale_of(b)).astype(BF)
        return carry

    lax.fori_loop(0, NB, scale_block, 0, unroll=4)
    greeted(peers)
    copies = Copies(send, recv)

    class Gather:
        def __init__(self, first, second, lo, n, chunks):
            self.f, self.s, self.chunks = first, second, chunks
            self.size = n // chunks
            self.at = [lo + i * self.size for i in range(chunks)]
            h = chunks // 2
            self.up_order = list(range(chunks))
            self.dn_order = list(range(chunks))[::-1]
            self.up_half = self.up_order[:h]
            self.dn_half = self.dn_order[: chunks - h]
            self.a, self.b = {}, {}

        def push(self, a, b, i, axis, step):
            at = self.at[i]
            ds = pl.ds(owner_at(self.f, a, self.s, b) * NB + at, self.size)
            return copies.start(gat.at[ds], gat.at[ds], {"rows": rank_along(axis, step)})

        def first_start(self):
            for u, d in zip(self.up_order, self.dn_order):
                self.a[-1, u] = self.push(0, 0, u, self.f, 1)
                self.a[1, d] = self.push(0, 0, d, self.f, -1)

        def first_forward(self, j, then=None):
            for side, order, half in ((-1, self.up_order, self.up_half), (1, self.dn_order, self.dn_half)):
                i = order[j]
                self.a[side, i].wait_recv()
                if i in half:
                    self.a[2 * side, i] = self.push(side, 0, i, self.f, -side)
                if then:
                    then(side, i)

        def far(self, j, then):
            for side, half in ((-1, self.up_half), (1, self.dn_half)):
                if j < len(half):
                    self.a[2 * side, half[j]].wait_recv()
                    then(2 * side, half[j])

        def second_start(self, a, i):
            self.b[a, -1, i] = self.push(a, 0, i, self.s, 1)
            self.b[a, 1, i] = self.push(a, 0, i, self.s, -1)

        def second_forward(self, a, i):
            side = -1 if i in self.up_half else 1
            self.b[a, side, i].wait_recv()
            last.append(self.push(a, side, i, self.s, -side))
            last.append(self.b[a, -side, i])

    PC, QC = 2, 2
    last = []
    gp = Gather("z", "x", 0, ZFIRST, PC)
    gq = Gather("x", "z", ZFIRST, NB - ZFIRST, QC)
    gp.first_start()
    gq.first_start()
    for i in range(PC):
        gp.second_start(0, i)
    for k, dev in devs:
        last.append(copies.start(cot.at[pl.ds(2 * k, 2)], cotx.at[c], dev))
    for cp in l_idx:
        cp.wait()
    tile_order(rowcol, count, idx_v)
    l_s = load(idx_v, idx)
    l_w.wait()
    wt[...] = w[...].T

    def turn(q):
        l_a[q].wait()

        def some(i, carry):
            for k in range(4):
                t = q * TC + i * 4 + k
                at[t] = a[t].T
            return carry

        lax.fori_loop(0, TC // 4, some, 0)

    for j in range(QC):
        gq.first_forward(j)
    turn(0)
    for j in range(PC):
        gp.first_forward(j, gp.second_start)
    for i in range(QC):
        gq.second_start(0, i)
    for i in range(PC):
        gp.second_forward(0, i)
    for j in range(QC):
        gq.second_start(-1, gq.up_order[j])
        gq.second_start(1, gq.dn_order[j])
    turn(1)
    for j in range((PC + 1) // 2):
        gp.far(j, gp.second_start)
    turn(2)
    for i in range(PC):
        gp.second_forward(-1, i)
        gp.second_forward(1, PC - 1 - i)
    turn(3)
    for i in range(QC):
        gq.second_forward(0, i)
    for j in range((QC + 1) // 2):
        gq.far(j, gq.second_start)
    for i in range(QC):
        gq.second_forward(-1, i)
        gq.second_forward(1, QC - 1 - i)
    for j in range((PC + 1) // 2):
        gp.second_forward(-2, gp.up_half[j])
        gp.second_forward(2, gp.dn_half[j])
    for j in range((QC + 1) // 2):
        gq.second_forward(-2, gq.up_half[j])
        gq.second_forward(2, gq.dn_half[j])
    for cp in last:
        cp.wait_recv()
    for cp in [l_s, l_cot]:
        cp.wait()

    sums[T] = jnp.zeros((FS, BLK), F32)

    def forward(i, run):
        for k in range(TB):
            p = i * TB + k
            m = lax.dot_general(
                gat[idx[COLP, p]], at[idx[PERM, p]], (((1,), (0,)), ((), ())), preferred_element_type=F32
            )
            same = idx[KEYP, p] == idx[KEYP, jnp.maximum(p - 1, 0)]
            run = jnp.where(same, run, 0.0) + m
            sums[p] = run
        return run

    lax.fori_loop(0, T // TB, forward, jnp.zeros((FS, BLK), F32))

    def finish_row(b, carry):
        hid[b] = (sums[idx[ROWEND, b]] * scale_of(b)).astype(BF)
        return carry

    lax.fori_loop(0, NB, finish_row, 0, unroll=4)

    arrivals = [
        copies.start(hid.at[pl.ds(2 * k, 2)], hx.at[c], dev)
        for k, dev in devs
    ]
    hx[c] = hid[pl.ds(2 * c, 2)]
    runs[T] = jnp.zeros((FS, BLK), BF)
    for cp in arrivals:
        cp.wait_recv()

    def wide(ref):
        return jnp.concatenate([ref[:, b].reshape(NC * FS, BLK) for b in range(2)], axis=1)

    def narrow(ref, value):
        for b in range(2):
            ref[:, b] = value[:, b * BLK : (b + 1) * BLK].reshape(NC, FS, BLK)

    def to_owner(src, dst):
        got = [
            copies.start(src.at[k], dst.at[pl.ds(2 * c, 2)], dev)
            for k, dev in devs
        ]
        return got, load(src.at[c], dst.at[pl.ds(2 * c, 2)])

    x = wide(hx)
    pre = jnp.dot(wt[...], x, preferred_element_type=F32)
    sig = jax.nn.sigmoid(pre)
    slope = (wide(cotx).astype(F32) * sig * (1.0 + pre * (1.0 - sig))).astype(BF)
    s = jnp.concatenate([scale_of(2 * c + b) for b in range(2)], axis=1)
    narrow(back_s, (jnp.dot(w[...], slope, preferred_element_type=F32) * s).astype(BF))
    got_b, mine_b = to_owner(back_s, back)
    narrow(act_s, (pre * sig).astype(BF))
    wg[...] = (
        lax.dot_general(x, slope, (((1,), (1,)), ((), ())), preferred_element_type=F32)
        .astype(BF)
        .reshape(wg.shape)
    )
    for cp in got_b:
        cp.wait_recv()
    mine_b.wait()

    def backward(i, run):
        for k in range(TB):
            t = i * TB + k
            m = jnp.dot(back[idx[ROW, t]], a[t], preferred_element_type=F32)
            same = idx[COL, t] == idx[COL, jnp.maximum(t - 1, 0)]
            run = jnp.where(same, run, 0.0) + m
            runs[t] = run.astype(BF)
        return run

    lax.fori_loop(0, T // TB, backward, jnp.zeros((FS, BLK), F32))

    def local(first, a, second, b, lo, n):
        return part.at[pl.ds(owner_at(first, a, second, b) * NB + lo, n)]

    def add_into(dst, p, q):
        def one(i, carry):
            dst[i] = (p[i].astype(F32) + q[i].astype(F32)).astype(BF)
            return carry

        lax.fori_loop(0, dst.shape[0], one, 0, unroll=2)

    class Ring:
        def __init__(self, axis, n, shard, land, work):
            self.n, self.h, self.shard, self.land, self.work = n, n // 2, shard, land, work
            self.up, self.dn = {"rows": rank_along(axis, 1)}, {"rows": rank_along(axis, -1)}
            self.got = []

        def far(self):
            n, h = self.n, self.h
            self.far_dn = copies.start(self.shard(-2).at[pl.ds(0, h)], self.land.at[pl.ds(0, h)], self.dn)
            self.far_up = copies.start(
                self.shard(2).at[pl.ds(h, n - h)], self.land.at[pl.ds(h, n - h)], self.up
            )

        def raw_dn(self):
            n, h = self.n, self.h
            self.got.append(
                copies.start(self.shard(-1).at[pl.ds(h, n - h)], self.land.at[pl.ds(n + h, n - h)], self.dn)
            )

        def raw_up(self):
            n, h = self.n, self.h
            self.got.append(
                copies.start(self.shard(1).at[pl.ds(0, h)], self.land.at[pl.ds(2 * n, h)], self.up)
            )

        def start(self):
            self.far()
            self.raw_dn()
            self.raw_up()

        def forward(self):
            n, h = self.n, self.h
            lo, hi = pl.ds(0, h), pl.ds(h, n - h)
            self.far_dn.wait_recv()
            add_into(self.work.at[lo], self.land.at[lo], self.shard(-1).at[lo])
            self.got.append(copies.start(self.work.at[lo], self.land.at[pl.ds(n, h)], self.dn))
            self.far_up.wait_recv()
            add_into(self.work.at[hi], self.land.at[hi], self.shard(1).at[hi])
            self.got.append(copies.start(self.work.at[hi], self.land.at[pl.ds(2 * n + h, n - h)], self.up))

        def end(self, store):
            n, land = self.n, self.land
            for cp in self.got:
                cp.wait_recv()
            mine = self.shard(0)

            def one(i, carry):
                store(i, mine[i].astype(F32) + land[n + i].astype(F32) + land[2 * n + i].astype(F32))
                return carry

            lax.fori_loop(0, n, one, 0, unroll=2)

    slot = {2: 0, -2: 0, -1: 1, 1: 2, 0: 3}

    def first_rings(first, second, lo, n):
        return {
            b: Ring(
                first,
                n,
                lambda a, b=b: local(first, a, second, b, lo, n),
                inner.at[slot[b], pl.ds(3 * lo, 3 * n)],
                half.at[slot[b], pl.ds(lo, n)],
            )
            for b in (2, -1, 1, 0)
        }

    def second_ring(second, lo, n):
        return Ring(
            second,
            n,
            lambda a: summed.at[slot[a], pl.ds(lo, n)],
            tail.at[pl.ds(3 * lo, 3 * n)],
            half.at[4, pl.ds(lo, n)],
        )

    def keep(b, lo):
        def store(j, v):
            summed[slot[b], lo + j] = v.astype(BF)

        return store

    def final(lo):
        def store(j, v):
            out[lo + j] = (v * scale_of(lo + j)).astype(BF)

        return store

    PN, QN = XFIRST, NB - XFIRST
    away = (2, -1, 1, 0)

    def pick(dx, dz, lo, n):
        first = owner_at("x", dx, "z", dz) * NB + lo

        def one(i, carry):
            part[first + i] = runs[idx[COLEND, first + i]]
            return carry

        lax.fori_loop(0, n, one, 0, unroll=True)

    rings, seconds = [], []
    for lo, n in ((0, 13), (13, 13)):
        one = first_rings("x", "z", lo, n)
        seconds.append(second_ring("z", lo, n))
        rings += [(one[b], b, lo, seconds[-1]) for b in away]
    q1, q2 = first_rings("z", "x", PN, QN), second_ring("x", PN, QN)

    def end_first(ring, b, lo, second):
        ring.end(keep(b, lo))
        if b == 2:
            second.far()
        if b == -1:
            second.raw_dn()
        if b == 1:
            second.raw_up()

    AHEAD = 3
    for dx in away:
        pick(dx, 2, 0, PN)
    rings[0][0].start()
    for dz in away:
        for dx in away:
            pick(dx, dz, PN, QN)
    for b in away:
        q1[b].start()
    for dz in away[1:]:
        for dx in away:
            pick(dx, dz, 0, PN)
    for k in range(1, AHEAD):
        rings[k][0].start()
    got_a, mine_a = to_owner(act_s, act)
    wys = [
        copies.start(wg.at[pl.ds(4 * ((y + k) % NY), 4)], wy.at[k - 1], d)
        for k, d in enumerate(ypeers, 1)
    ]

    def sum_y():
        for cp in wys:
            cp.wait_recv()
        for j in range(4):
            v = wg[4 * y + j].astype(F32)
            for k in range(NY - 1):
                v = v + wy[k, j].astype(F32)
            ws[j] = v.astype(BF)
        return [copies.start(ws.at[2 * q + 1 - core], wc.at[q], cpeer) for q in range(2)]

    def sum_core():
        for cp in wcs:
            cp.wait_recv()
        for q in range(2):
            wm[q] = (ws[2 * q + core].astype(F32) + wc[q].astype(F32)).astype(BF)
        return copies.start(wm.at[1 - zl], wz, zpeer)

    def sum_near():
        wzc.wait_recv()
        w1[...] = (wm[zl].astype(F32) + wz[...].astype(F32)).astype(BF)
        return [copies.start(w1, wx.at[k], d) for k, d in enumerate(xs)]

    def sum_x():
        for cp in wxs:
            cp.wait_recv()
        v = w1[...].astype(F32)
        for k in range(NX - 1):
            v = v + wx[k].astype(F32)
        w2[...] = v.astype(BF)
        return [copies.start(w2, wv.at[k], d) for k, d in enumerate(zs)]

    for i in range(len(rings)):
        rings[i][0].forward()
        if i + AHEAD < len(rings):
            rings[i + AHEAD][0].start()
        if i >= 1:
            end_first(*rings[i - 1])
            if rings[i - 1][1] == 1:
                rings[i - 1][3].forward()
        if i == 0:
            q1[2].forward()
        if i == 1:
            q1[-1].forward()
            q1[1].forward()
            q1[0].forward()
        if i == 2:
            wcs = sum_y()
        if i == 3:
            wzc = sum_core()
            end_first(q1[2], 2, PN, q2)
        if i == 4:
            end_first(q1[-1], -1, PN, q2)
            end_first(q1[1], 1, PN, q2)
            q1[0].end(keep(0, PN))
            wxs = sum_near()
        if i == 5:
            q2.forward()
            wvs = sum_x()
        if i == 6:
            seconds[0].end(final(0))
            q2.end(final(PN))
    for cp in wvs:
        cp.wait_recv()
    v = w2[...].astype(F32)
    for k in range(NZ - 1):
        v = v + wv[k].astype(F32)
    wout[...] = v
    end_first(*rings[-1])
    seconds[1].end(final(13))
    for cp in got_a:
        cp.wait_recv()
    mine_a.wait()
    copies.finish()


def hand_over_kernel(a_in, b_in, c_in, a_out, b_out, c_out, sem):
    moves = [
        pltpu.make_async_copy(src, dst, sem.at[i])
        for i, (src, dst) in enumerate(((a_in, a_out), (b_in, b_out), (c_in, c_out)))
    ]
    for m in moves:
        m.start()
    for m in moves:
        m.wait()


def hand_over(results):
    vm = pl.BlockSpec(memory_space=pltpu.VMEM)
    hb = pl.BlockSpec(memory_space=pl.ANY)
    return pl.pallas_call(
        hand_over_kernel,
        name="hand_over",
        out_shape=tuple(jax.ShapeDtypeStruct(r.shape, r.dtype) for r in results),
        in_specs=[vm] * 3,
        out_specs=(hb,) * 3,
        scratch_shapes=[pltpu.SemaphoreType.DMA((3,))],
        compiler_params=pltpu.CompilerParams(vmem_limit_bytes=60 << 20),
    )(*results)


N_COPIES = 2 * 2 * 15 + 4 * (NC - 1) + 3 * (4 * 6 + 6) + (NY - 1) + 2 + 1 + (NX - 1) + (NZ - 1)


def body(features, cotangent, weight, degree, tile_row, tile_col, tile_count, tile_weights):
    hb = pl.BlockSpec(memory_space=pl.ANY)
    vm = pl.BlockSpec(memory_space=pltpu.VMEM)
    sm = pl.BlockSpec(memory_space=pltpu.SMEM)
    f = weight.shape[1]
    shard = (FS, BLK)
    results = pl.pallas_call(
        layer_kernel,
        name="layer",
        out_shape=(
            jax.ShapeDtypeStruct((NB,) + shard, BF),
            jax.ShapeDtypeStruct((NB,) + shard, BF),
            jax.ShapeDtypeStruct((FS, f), F32),
        ),
        in_specs=[hb, hb, hb, hb, hb, hb, sm, hb],
        out_specs=(hb, vm, vm),
        scratch_shapes=[
            pltpu.VMEM((NB,) + shard, BF),
            pltpu.VMEM((NB, BLK), jnp.int32),
            pltpu.VMEM(weight.shape, BF),
            pltpu.VMEM(weight.shape, BF),
            pltpu.VMEM((2, 1, T), jnp.int32),
            pltpu.VMEM((T, BLK, BLK), BF),
            pltpu.VMEM((T, BLK, BLK), BF),
            pltpu.VMEM((8, NR * NB), jnp.int32),
            pltpu.SMEM((8, NR * NB), jnp.int32),
            pltpu.VMEM((NR * NB,) + shard, BF),
            pltpu.VMEM((NC, 2) + shard, BF),
            pltpu.VMEM((T + 1,) + shard, F32),
            pltpu.VMEM((NB,) + shard, BF),
            pltpu.VMEM((NC, 2) + shard, BF),
            pltpu.VMEM((NC, 2) + shard, BF),
            pltpu.VMEM((NC, 2) + shard, BF),
            pltpu.VMEM((NB,) + shard, BF),
            pltpu.VMEM((T + 1,) + shard, BF),
            pltpu.VMEM((NR * NB,) + shard, BF),
            pltpu.VMEM((NC, FS, f), BF),
            pltpu.VMEM((4, 3 * NB) + shard, BF),
            pltpu.VMEM((4, NB) + shard, BF),
            pltpu.VMEM((5, NB) + shard, BF),
            pltpu.VMEM((3 * NB,) + shard, BF),
            pltpu.VMEM((NY - 1, 4, FS, f), BF),
            pltpu.VMEM((4, FS, f), BF),
            pltpu.VMEM((2, FS, f), BF),
            pltpu.VMEM((2, FS, f), BF),
            pltpu.VMEM((FS, f), BF),
            pltpu.VMEM((FS, f), BF),
            pltpu.VMEM((NX - 1, FS, f), BF),
            pltpu.VMEM((FS, f), BF),
            pltpu.VMEM((NZ - 1, FS, f), BF),
            pltpu.SemaphoreType.DMA((N_COPIES,)),
            pltpu.SemaphoreType.DMA((N_COPIES,)),
            pltpu.SemaphoreType.DMA((16,)),
        ],
        compiler_params=pltpu.CompilerParams(
            collective_id=0, has_side_effects=True, vmem_limit_bytes=60 << 20
        ),
    )(
        features,
        cotangent,
        weight,
        degree,
        tile_row.reshape(1, T),
        tile_col.reshape(1, T),
        tile_count,
        tile_weights,
    )
    return hand_over(results)


def solution(mesh):
    in_specs = (
        P("rows", "cols", None),
        P("rows", "cols", None),
        P(),
        P("rows", None),
        P("rows"),
        P("rows"),
        P("rows"),
        P("rows", None, None),
    )
    out_specs = (P("rows", "cols", None), P("rows", "cols", None), P("cols", None))
    return jax.shard_map(body, mesh=mesh, in_specs=in_specs, out_specs=out_specs, check_vma=False)
```

```python
import functools

import jax
import jax.numpy as jnp
from jax import lax
from jax.experimental import pallas as pl
from jax.experimental.pallas import tpu as pltpu
from jax.sharding import PartitionSpec as P

BF = jnp.bfloat16
F32 = jnp.float32
NB = 32
FS = 32
BLK = 128
NX = 4
NZ = 4
NR = NX * NZ
NY = 4
NC = 16
ZFIRST = 26
XFIRST = 26
TC = 64
TB = 128
T = 256
DEAD = 1024


def rank_along(axis, step):
    r = lax.axis_index("rows")
    x, z = r // NZ, r % NZ
    if axis == "x":
        return ((x + step + NX) % NX) * NZ + z
    return x * NZ + (z + step + NZ) % NZ


def owner_at(first, a, second, b):
    r = lax.axis_index("rows")
    step = {first: a, second: b}
    return ((r // NZ + step["x"] + NX) % NX) * NZ + (r % NZ + step["z"] + NZ) % NZ


class Copies:
    def __init__(self, send, recv):
        self.send, self.recv, self.n, self.started = send, recv, 0, []

    def start(self, src, dst, device):
        k = self.n
        self.n += 1
        c = pltpu.make_async_remote_copy(
            src_ref=src,
            dst_ref=dst,
            send_sem=self.send.at[k],
            recv_sem=self.recv.at[k],
            device_id=device,
            device_id_type=pl.DeviceIdType.MESH,
        )
        c.start()
        self.started.append(c)
        return c

    def finish(self):
        for c in self.started:
            c.wait_send()


def greet(devices):
    barrier = pltpu.get_barrier_semaphore()
    for d in devices:
        pl.semaphore_signal(barrier, inc=1, device_id=d, device_id_type=pl.DeviceIdType.MESH)


def greeted(devices):
    pl.semaphore_wait(pltpu.get_barrier_semaphore(), len(devices))


def other_cols():
    c = lax.axis_index("cols")
    y, z, core = c // 4, (c // 2) % 2, c % 2
    found = []
    for dy in (2, 1, 3, 0):
        for dz in (1, 0):
            for dc in (1, 0):
                if (dy, dz, dc) != (0, 0, 0):
                    k = ((y + dy) % NY) * 4 + (z + dz - 2 * z * dz) * 2 + core + dc - 2 * core * dc
                    found.append((k, {"cols": k}))
    return found


PERM, COLP, KEYP, ROW, COL, COLEND, ROWEND = range(7)


def tile_order(rowcol, count, idx_v):
    i32 = jnp.int32
    lane = lax.broadcasted_iota(i32, (1, T), 1)
    live = lane < count[0]
    row, col = rowcol[0], rowcol[1]
    key = jnp.where(live, row, DEAD)
    ckey = jnp.where(live, col, DEAD)

    def down(v):
        return jnp.broadcast_to(v, (8, T)).T[:, :1]

    def total(mask):
        return jnp.sum(mask.astype(i32), axis=0, keepdims=True)

    key_d, col_d, ckey_d = down(key), down(col), down(ckey)
    sub = lax.broadcasted_iota(i32, (T, T), 0)
    across = lax.broadcasted_iota(i32, (T, T), 1)
    pos = total((key_d < key) | ((key_d == key) & (sub < across)))
    here = down(pos) == across

    def sorted_(v_d):
        return jnp.sum(jnp.where(here, v_d, 0), axis=0, keepdims=True)

    def ends(v_d, n):
        b = lax.broadcasted_iota(i32, (T, n), 1)
        return jnp.where(total(v_d == b) > 0, total(v_d <= b) - 1, T)

    idx_v[pl.ds(PERM, 1), :T] = sorted_(sub)
    idx_v[pl.ds(COLP, 1), :T] = sorted_(col_d)
    idx_v[pl.ds(KEYP, 1), :T] = sorted_(key_d)
    idx_v[pl.ds(ROW, 1), :T] = row
    idx_v[pl.ds(COL, 1), :T] = ckey
    idx_v[pl.ds(COLEND, 1), :] = ends(ckey_d, NR * NB)
    idx_v[pl.ds(ROWEND, 1), :BLK] = ends(key_d, BLK)


def layer_kernel(
    feat, cot, w_h, deg_h, row_h, col_h, count, a_h,
    act, out, wout,
    fbuf, deg, w, wt, rowcol, a, at, idx_v, idx, gat, cotx, sums, hid, hx, act_s, back_s, back, runs, part, wg,
    inner, summed, half, tail, wy, ws, wc, wm, wz, w1, wx, w2, wv,
    send, recv, lsem,
):
    me = lax.axis_index("rows")
    c = lax.axis_index("cols")
    y, low = c // 4, c % 4
    zl, core = low // 2, low % 2
    devs = other_cols()
    ypeers = [{"cols": ((y + k) % NY) * 4 + low} for k in range(1, NY)]
    cpeer = {"cols": c + 1 - 2 * core}
    zpeer = {"cols": c + 2 - 4 * zl}
    xs = [{"rows": rank_along("x", k)} for k in range(1, NX)]
    zs = [{"rows": rank_along("z", k)} for k in range(1, NZ)]
    peers = [d for _, d in devs] + xs + zs
    greet(peers)
    loads = []

    def load(src, dst):
        cp = pltpu.make_async_copy(src, dst, lsem.at[len(loads)])
        cp.start()
        loads.append(cp)
        return cp

    l_feat = load(feat, fbuf)
    l_deg = load(deg_h, deg)
    l_idx = [load(row_h, rowcol.at[0]), load(col_h, rowcol.at[1])]
    l_w = load(w_h, w)
    l_cot = load(cot.at[pl.ds(2 * c, 2)], cotx.at[c])
    l_a = [load(a_h.at[pl.ds(i * T // 4, T // 4)], a.at[pl.ds(i * T // 4, T // 4)]) for i in range(4)]
    l_feat.wait()
    l_deg.wait()

    def scale_of(b):
        return lax.rsqrt(deg[pl.ds(b, 1), :].astype(F32))

    def scale_block(b, carry):
        gat[me * NB + b] = (fbuf[b].astype(F32) * scale_of(b)).astype(BF)
        return carry

    lax.fori_loop(0, NB, scale_block, 0, unroll=4)
    greeted(peers)
    copies = Copies(send, recv)

    class Gather:
        def __init__(self, first, second, lo, n, chunks):
            self.f, self.s, self.chunks = first, second, chunks
            self.size = n // chunks
            self.at = [lo + i * self.size for i in range(chunks)]
            h = chunks // 2
            self.up_order = list(range(chunks))
            self.dn_order = list(range(chunks))[::-1]
            self.up_half = self.up_order[:h]
            self.dn_half = self.dn_order[: chunks - h]
            self.a, self.b = {}, {}

        def push(self, a, b, i, axis, step):
            at = self.at[i]
            ds = pl.ds(owner_at(self.f, a, self.s, b) * NB + at, self.size)
            return copies.start(gat.at[ds], gat.at[ds], {"rows": rank_along(axis, step)})

        def first_start(self):
            for u, d in zip(self.up_order, self.dn_order):
                self.a[-1, u] = self.push(0, 0, u, self.f, 1)
                self.a[1, d] = self.push(0, 0, d, self.f, -1)

        def first_forward(self, j, then=None):
            for side, order, half in ((-1, self.up_order, self.up_half), (1, self.dn_order, self.dn_half)):
                i = order[j]
                self.a[side, i].wait_recv()
                if i in half:
                    self.a[2 * side, i] = self.push(side, 0, i, self.f, -side)
                if then:
                    then(side, i)

        def far(self, j, then):
            for side, half in ((-1, self.up_half), (1, self.dn_half)):
                if j < len(half):
                    self.a[2 * side, half[j]].wait_recv()
                    then(2 * side, half[j])

        def second_start(self, a, i):
            self.b[a, -1, i] = self.push(a, 0, i, self.s, 1)
            self.b[a, 1, i] = self.push(a, 0, i, self.s, -1)

        def second_forward(self, a, i):
            side = -1 if i in self.up_half else 1
            self.b[a, side, i].wait_recv()
            last.append(self.push(a, side, i, self.s, -side))
            last.append(self.b[a, -side, i])

    PC, QC = 2, 2
    last = []
    gp = Gather("z", "x", 0, ZFIRST, PC)
    gq = Gather("x", "z", ZFIRST, NB - ZFIRST, QC)
    gp.first_start()
    gq.first_start()
    for i in range(PC):
        gp.second_start(0, i)
    for k, dev in devs:
        last.append(copies.start(cot.at[pl.ds(2 * k, 2)], cotx.at[c], dev))
    for cp in l_idx:
        cp.wait()
    tile_order(rowcol, count, idx_v)
    l_s = load(idx_v, idx)
    l_w.wait()
    wt[...] = w[...].T

    def turn(q):
        l_a[q].wait()

        def some(i, carry):
            for k in range(4):
                t = q * TC + i * 4 + k
                at[t] = a[t].T
            return carry

        lax.fori_loop(0, TC // 4, some, 0)

    for j in range(QC):
        gq.first_forward(j)
    turn(0)
    for j in range(PC):
        gp.first_forward(j, gp.second_start)
    for i in range(QC):
        gq.second_start(0, i)
    for i in range(PC):
        gp.second_forward(0, i)
    for j in range(QC):
        gq.second_start(-1, gq.up_order[j])
        gq.second_start(1, gq.dn_order[j])
    turn(1)
    for j in range((PC + 1) // 2):
        gp.far(j, gp.second_start)
    turn(2)
    for i in range(PC):
        gp.second_forward(-1, i)
        gp.second_forward(1, PC - 1 - i)
    turn(3)
    for i in range(QC):
        gq.second_forward(0, i)
    for j in range((QC + 1) // 2):
        gq.far(j, gq.second_start)
    for i in range(QC):
        gq.second_forward(-1, i)
        gq.second_forward(1, QC - 1 - i)
    for j in range((PC + 1) // 2):
        gp.second_forward(-2, gp.up_half[j])
        gp.second_forward(2, gp.dn_half[j])
    for j in range((QC + 1) // 2):
        gq.second_forward(-2, gq.up_half[j])
        gq.second_forward(2, gq.dn_half[j])
    for cp in last:
        cp.wait_recv()
    for cp in [l_s, l_cot]:
        cp.wait()

    sums[T] = jnp.zeros((FS, BLK), F32)

    def forward(i, run):
        for k in range(TB):
            p = i * TB + k
            m = lax.dot_general(
                gat[idx[COLP, p]], at[idx[PERM, p]], (((1,), (0,)), ((), ())), preferred_element_type=F32
            )
            same = idx[KEYP, p] == idx[KEYP, jnp.maximum(p - 1, 0)]
            run = jnp.where(same, run, 0.0) + m
            sums[p] = run
        return run

    lax.fori_loop(0, T // TB, forward, jnp.zeros((FS, BLK), F32))

    def finish_row(b, carry):
        hid[b] = (sums[idx[ROWEND, b]] * scale_of(b)).astype(BF)
        return carry

    lax.fori_loop(0, NB, finish_row, 0, unroll=4)

    arrivals = [
        copies.start(hid.at[pl.ds(2 * k, 2)], hx.at[c], dev)
        for k, dev in devs
    ]
    hx[c] = hid[pl.ds(2 * c, 2)]
    runs[T] = jnp.zeros((FS, BLK), BF)
    for cp in arrivals:
        cp.wait_recv()

    def wide(ref):
        return jnp.concatenate([ref[:, b].reshape(NC * FS, BLK) for b in range(2)], axis=1)

    def narrow(ref, value):
        for b in range(2):
            ref[:, b] = value[:, b * BLK : (b + 1) * BLK].reshape(NC, FS, BLK)

    def to_owner(src, dst):
        got = [
            copies.start(src.at[k], dst.at[pl.ds(2 * c, 2)], dev)
            for k, dev in devs
        ]
        return got, load(src.at[c], dst.at[pl.ds(2 * c, 2)])

    x = wide(hx)
    pre = jnp.dot(wt[...], x, preferred_element_type=F32)
    sig = jax.nn.sigmoid(pre)
    slope = (wide(cotx).astype(F32) * sig * (1.0 + pre * (1.0 - sig))).astype(BF)
    s = jnp.concatenate([scale_of(2 * c + b) for b in range(2)], axis=1)
    narrow(back_s, (jnp.dot(w[...], slope, preferred_element_type=F32) * s).astype(BF))
    got_b, mine_b = to_owner(back_s, back)
    narrow(act_s, (pre * sig).astype(BF))
    wg[...] = (
        lax.dot_general(x, slope, (((1,), (1,)), ((), ())), preferred_element_type=F32)
        .astype(BF)
        .reshape(wg.shape)
    )
    for cp in got_b:
        cp.wait_recv()
    mine_b.wait()

    def backward(i, run):
        for k in range(TB):
            t = i * TB + k
            m = jnp.dot(back[idx[ROW, t]], a[t], preferred_element_type=F32)
            same = idx[COL, t] == idx[COL, jnp.maximum(t - 1, 0)]
            run = jnp.where(same, run, 0.0) + m
            runs[t] = run.astype(BF)
        return run

    lax.fori_loop(0, T // TB, backward, jnp.zeros((FS, BLK), F32))

    def local(first, a, second, b, lo, n):
        return part.at[pl.ds(owner_at(first, a, second, b) * NB + lo, n)]

    def add_into(dst, p, q):
        def one(i, carry):
            dst[i] = (p[i].astype(F32) + q[i].astype(F32)).astype(BF)
            return carry

        lax.fori_loop(0, dst.shape[0], one, 0, unroll=2)

    class Ring:
        def __init__(self, axis, n, shard, land, work):
            self.n, self.h, self.shard, self.land, self.work = n, n // 2, shard, land, work
            self.up, self.dn = {"rows": rank_along(axis, 1)}, {"rows": rank_along(axis, -1)}
            self.got = []

        def far(self):
            n, h = self.n, self.h
            self.far_dn = copies.start(self.shard(-2).at[pl.ds(0, h)], self.land.at[pl.ds(0, h)], self.dn)
            self.far_up = copies.start(
                self.shard(2).at[pl.ds(h, n - h)], self.land.at[pl.ds(h, n - h)], self.up
            )

        def raw_dn(self):
            n, h = self.n, self.h
            self.got.append(
                copies.start(self.shard(-1).at[pl.ds(h, n - h)], self.land.at[pl.ds(n + h, n - h)], self.dn)
            )

        def raw_up(self):
            n, h = self.n, self.h
            self.got.append(
                copies.start(self.shard(1).at[pl.ds(0, h)], self.land.at[pl.ds(2 * n, h)], self.up)
            )

        def start(self):
            self.far()
            self.raw_dn()
            self.raw_up()

        def forward(self):
            n, h = self.n, self.h
            lo, hi = pl.ds(0, h), pl.ds(h, n - h)
            self.far_dn.wait_recv()
            add_into(self.work.at[lo], self.land.at[lo], self.shard(-1).at[lo])
            self.got.append(copies.start(self.work.at[lo], self.land.at[pl.ds(n, h)], self.dn))
            self.far_up.wait_recv()
            add_into(self.work.at[hi], self.land.at[hi], self.shard(1).at[hi])
            self.got.append(copies.start(self.work.at[hi], self.land.at[pl.ds(2 * n + h, n - h)], self.up))

        def end(self, store):
            n, land = self.n, self.land
            for cp in self.got:
                cp.wait_recv()
            mine = self.shard(0)

            def one(i, carry):
                store(i, mine[i].astype(F32) + land[n + i].astype(F32) + land[2 * n + i].astype(F32))
                return carry

            lax.fori_loop(0, n, one, 0, unroll=2)

    slot = {2: 0, -2: 0, -1: 1, 1: 2, 0: 3}

    def first_rings(first, second, lo, n):
        return {
            b: Ring(
                first,
                n,
                lambda a, b=b: local(first, a, second, b, lo, n),
                inner.at[slot[b], pl.ds(3 * lo, 3 * n)],
                half.at[slot[b], pl.ds(lo, n)],
            )
            for b in (2, -1, 1, 0)
        }

    def second_ring(second, lo, n):
        return Ring(
            second,
            n,
            lambda a: summed.at[slot[a], pl.ds(lo, n)],
            tail.at[pl.ds(3 * lo, 3 * n)],
            half.at[4, pl.ds(lo, n)],
        )

    def keep(b, lo):
        def store(j, v):
            summed[slot[b], lo + j] = v.astype(BF)

        return store

    def final(lo):
        def store(j, v):
            out[lo + j] = (v * scale_of(lo + j)).astype(BF)

        return store

    PN, QN = XFIRST, NB - XFIRST
    away = (2, -1, 1, 0)

    def pick(dx, dz, lo, n):
        first = owner_at("x", dx, "z", dz) * NB + lo

        def one(i, carry):
            part[first + i] = runs[idx[COLEND, first + i]]
            return carry

        lax.fori_loop(0, n, one, 0, unroll=True)

    rings, seconds = [], []
    for lo, n in ((0, 13), (13, 13)):
        one = first_rings("x", "z", lo, n)
        seconds.append(second_ring("z", lo, n))
        rings += [(one[b], b, lo, seconds[-1]) for b in away]
    q1, q2 = first_rings("z", "x", PN, QN), second_ring("x", PN, QN)

    def end_first(ring, b, lo, second):
        ring.end(keep(b, lo))
        if b == 2:
            second.far()
        if b == -1:
            second.raw_dn()
        if b == 1:
            second.raw_up()

    AHEAD = 3
    for dx in away:
        pick(dx, 2, 0, PN)
    rings[0][0].start()
    for dz in away:
        for dx in away:
            pick(dx, dz, PN, QN)
    for b in away:
        q1[b].start()
    for dz in away[1:]:
        for dx in away:
            pick(dx, dz, 0, PN)
    for k in range(1, AHEAD):
        rings[k][0].start()
    got_a, mine_a = to_owner(act_s, act)
    wys = [
        copies.start(wg.at[pl.ds(4 * ((y + k) % NY), 4)], wy.at[k - 1], d)
        for k, d in enumerate(ypeers, 1)
    ]

    def sum_y():
        for cp in wys:
            cp.wait_recv()
        for j in range(4):
            v = wg[4 * y + j].astype(F32)
            for k in range(NY - 1):
                v = v + wy[k, j].astype(F32)
            ws[j] = v.astype(BF)
        return [copies.start(ws.at[2 * q + 1 - core], wc.at[q], cpeer) for q in range(2)]

    def sum_core():
        for cp in wcs:
            cp.wait_recv()
        for q in range(2):
            wm[q] = (ws[2 * q + core].astype(F32) + wc[q].astype(F32)).astype(BF)
        return copies.start(wm.at[1 - zl], wz, zpeer)

    def sum_near():
        wzc.wait_recv()
        w1[...] = (wm[zl].astype(F32) + wz[...].astype(F32)).astype(BF)
        return [copies.start(w1, wx.at[k], d) for k, d in enumerate(xs)]

    def sum_x():
        for cp in wxs:
            cp.wait_recv()
        v = w1[...].astype(F32)
        for k in range(NX - 1):
            v = v + wx[k].astype(F32)
        w2[...] = v.astype(BF)
        return [copies.start(w2, wv.at[k], d) for k, d in enumerate(zs)]

    for i in range(len(rings)):
        rings[i][0].forward()
        if i + AHEAD < len(rings):
            rings[i + AHEAD][0].start()
        if i >= 1:
            end_first(*rings[i - 1])
            if rings[i - 1][1] == 1:
                rings[i - 1][3].forward()
        if i == 0:
            q1[2].forward()
        if i == 1:
            q1[-1].forward()
            q1[1].forward()
            q1[0].forward()
        if i == 2:
            wcs = sum_y()
        if i == 3:
            wzc = sum_core()
            end_first(q1[2], 2, PN, q2)
        if i == 4:
            end_first(q1[-1], -1, PN, q2)
            end_first(q1[1], 1, PN, q2)
            q1[0].end(keep(0, PN))
            wxs = sum_near()
        if i == 5:
            q2.forward()
            wvs = sum_x()
        if i == 6:
            seconds[0].end(final(0))
            q2.end(final(PN))
    for cp in wvs:
        cp.wait_recv()
    v = w2[...].astype(F32)
    for k in range(NZ - 1):
        v = v + wv[k].astype(F32)
    wout[...] = v
    end_first(*rings[-1])
    seconds[1].end(final(13))
    for cp in got_a:
        cp.wait_recv()
    mine_a.wait()
    copies.finish()


def hand_over_kernel(a_in, b_in, c_in, a_out, b_out, c_out, sem):
    moves = [
        pltpu.make_async_copy(src, dst, sem.at[i])
        for i, (src, dst) in enumerate(((a_in, a_out), (b_in, b_out), (c_in, c_out)))
    ]
    for m in moves:
        m.start()
    for m in moves:
        m.wait()


def hand_over(results):
    vm = pl.BlockSpec(memory_space=pltpu.VMEM)
    hb = pl.BlockSpec(memory_space=pl.ANY)
    return pl.pallas_call(
        hand_over_kernel,
        name="hand_over",
        out_shape=tuple(jax.ShapeDtypeStruct(r.shape, r.dtype) for r in results),
        in_specs=[vm] * 3,
        out_specs=(hb,) * 3,
        scratch_shapes=[pltpu.SemaphoreType.DMA((3,))],
        compiler_params=pltpu.CompilerParams(vmem_limit_bytes=60 << 20),
    )(*results)


N_COPIES = 2 * 2 * 15 + 4 * (NC - 1) + 3 * (4 * 6 + 6) + (NY - 1) + 2 + 1 + (NX - 1) + (NZ - 1)


def body(features, cotangent, weight, degree, tile_row, tile_col, tile_count, tile_weights):
    hb = pl.BlockSpec(memory_space=pl.ANY)
    vm = pl.BlockSpec(memory_space=pltpu.VMEM)
    sm = pl.BlockSpec(memory_space=pltpu.SMEM)
    f = weight.shape[1]
    shard = (FS, BLK)
    results = pl.pallas_call(
        layer_kernel,
        name="layer",
        out_shape=(
            jax.ShapeDtypeStruct((NB,) + shard, BF),
            jax.ShapeDtypeStruct((NB,) + shard, BF),
            jax.ShapeDtypeStruct((FS, f), F32),
        ),
        in_specs=[hb, hb, hb, hb, hb, hb, sm, hb],
        out_specs=(hb, vm, vm),
        scratch_shapes=[
            pltpu.VMEM((NB,) + shard, BF),
            pltpu.VMEM((NB, BLK), jnp.int32),
            pltpu.VMEM(weight.shape, BF),
            pltpu.VMEM(weight.shape, BF),
            pltpu.VMEM((2, 1, T), jnp.int32),
            pltpu.VMEM((T, BLK, BLK), BF),
            pltpu.VMEM((T, BLK, BLK), BF),
            pltpu.VMEM((8, NR * NB), jnp.int32),
            pltpu.SMEM((8, NR * NB), jnp.int32),
            pltpu.VMEM((NR * NB,) + shard, BF),
            pltpu.VMEM((NC, 2) + shard, BF),
            pltpu.VMEM((T + 1,) + shard, F32),
            pltpu.VMEM((NB,) + shard, BF),
            pltpu.VMEM((NC, 2) + shard, BF),
            pltpu.VMEM((NC, 2) + shard, BF),
            pltpu.VMEM((NC, 2) + shard, BF),
            pltpu.VMEM((NB,) + shard, BF),
            pltpu.VMEM((T + 1,) + shard, BF),
            pltpu.VMEM((NR * NB,) + shard, BF),
            pltpu.VMEM((NC, FS, f), BF),
            pltpu.VMEM((4, 3 * NB) + shard, BF),
            pltpu.VMEM((4, NB) + shard, BF),
            pltpu.VMEM((5, NB) + shard, BF),
            pltpu.VMEM((3 * NB,) + shard, BF),
            pltpu.VMEM((NY - 1, 4, FS, f), BF),
            pltpu.VMEM((4, FS, f), BF),
            pltpu.VMEM((2, FS, f), BF),
            pltpu.VMEM((2, FS, f), BF),
            pltpu.VMEM((FS, f), BF),
            pltpu.VMEM((FS, f), BF),
            pltpu.VMEM((NX - 1, FS, f), BF),
            pltpu.VMEM((FS, f), BF),
            pltpu.VMEM((NZ - 1, FS, f), BF),
            pltpu.SemaphoreType.DMA((N_COPIES,)),
            pltpu.SemaphoreType.DMA((N_COPIES,)),
            pltpu.SemaphoreType.DMA((16,)),
        ],
        compiler_params=pltpu.CompilerParams(
            collective_id=0, has_side_effects=True, vmem_limit_bytes=60 << 20
        ),
    )(
        features,
        cotangent,
        weight,
        degree,
        tile_row.reshape(1, T),
        tile_col.reshape(1, T),
        tile_count,
        tile_weights,
    )
    return hand_over(results)


def solution(mesh):
    in_specs = (
        P("rows", "cols", None),
        P("rows", "cols", None),
        P(),
        P("rows", None),
        P("rows"),
        P("rows"),
        P("rows"),
        P("rows", None, None),
    )
    out_specs = (P("rows", "cols", None), P("rows", "cols", None), P("cols", None))
    return jax.shard_map(body, mesh=mesh, in_specs=in_specs, out_specs=out_specs, check_vma=False)
```
